32 devices in a mesh: angle: 2 (over x), gx: 8 (over z, y), gy: 2 (over core).
Axes of the slice: x: 2, y: 2, z: 4, core: 2. Of those that a mesh axis runs over, the one named last changes fastest.
Arguments:
- electric: float32 [4, 3, 32, 64, 256], P('angle', None, 'gx', 'gy'), parts along dimension 0, may hold values from -3 to 3
- magnetic: float32 [4, 3, 32, 64, 256], P('angle', None, 'gx', 'gy'), parts along dimension 0, may hold values from -3 to 3
- polarize: float32 [4, 3, 32, 64, 256], P('angle', None, 'gx', 'gy'), parts along dimension 0, may hold values from -1.5 to 1.5
- currents: float32 [4, 3, 32, 64, 256], P('angle', None, 'gx', 'gy'), parts along dimension 0, may hold values from -1.5 to 1.5
- material: int32 [32, 64, 256], P('gx', 'gy'), may hold values from 0 to 7
- pole_of: int32 [8], replicated, may hold values from 0 to 3
- eps_inf: float32 [8], replicated, may hold values from 1 to 1.2
- pole_decay: float32 [4], replicated, may hold values from 0.5 to 0.95
- pole_freq: float32 [4], replicated, may hold values from 0.05 to 0.2
- pole_strength: float32 [4], replicated, may hold values from 0.3 to 2
- bloch: float32 [4], P('angle'), parts along dimension 0, may hold values from -3.140625 to 3.140625
Outputs:
- electric_out: float32 [4, 3, 32, 64, 256], P('angle', None, 'gx', 'gy'), parts along dimension 0
- magnetic_out: float32 [4, 3, 32, 64, 256], P('angle', None, 'gx', 'gy'), parts along dimension 0
- polar_out: float32 [4, 3, 32, 64, 256], P('angle', None, 'gx', 'gy'), parts along dimension 0
- current_out: float32 [4, 3, 32, 64, 256], P('angle', None, 'gx', 'gy'), parts along dimension 0
- harmonics: float32 [4, 8, 8, 32], P('angle', None, None, 'gx'), parts along dimension 0
The draws below stay inside these ranges and needn't reach their ends.
There are 2 independent parts, one for each index of `angle`. The reference program is written for one: setup_inputs(seed, part) draws one part's arguments, and reference() takes and returns one part's arrays. A program takes and returns all parts, laid end to end along the dimension named above; an argument that names none is the same for every part. Nothing has to cross between parts.
All inputs are finite; a program needn't handle non-finite values.
Results may differ from the reference program's by a relative error of at most 0.0003.
Values sent between devices are 32-bit elements; how exact they have to be, the bound alone decides.
No kernel may reach another device: no remote copies, remote signals or barrier semaphores. Data moves between devices by JAX's collectives and lax.ppermute only.
A program may use at most 128 MiB of HBM per device.

```python
import math
import jax
import jax.numpy as jnp
from jax import lax

NZ = 256
STEPS = 8
HARM = 8
MATS = 8
POLES = 4
NX = 32
NY = 64


def checker_sign():
    xcoords = jnp.arange(NX).astype(jnp.int32)
    ycoords = jnp.arange(NY).astype(jnp.int32)
    parity = (xcoords[:, None] + ycoords[None, :]) % 2
    return (1 - 2 * parity).astype(jnp.float32)[:, :, None]


def normal_part(key):
    return jnp.clip(jax.random.normal(key, (2, 3, NX, NY, NZ), jnp.float32), -4.0, 4.0)


def draw_electric(key, part):
    own_key = jax.random.fold_in(key, 101)
    values = 1.0 + 0.5 * normal_part(own_key)
    return (checker_sign() * values).astype(jnp.float32)


def draw_magnetic(key, part):
    own_key = jax.random.fold_in(key, 202)
    values = 1.0 + 0.5 * normal_part(own_key)
    return (checker_sign() * values).astype(jnp.float32)


def draw_polarize(key, part):
    own_key = jax.random.fold_in(key, 303)
    values = 0.5 + 0.25 * normal_part(own_key)
    return (checker_sign() * values).astype(jnp.float32)


def draw_currents(key, part):
    own_key = jax.random.fold_in(key, 404)
    values = 0.5 + 0.25 * normal_part(own_key)
    return (checker_sign() * values).astype(jnp.float32)


def with_ends(drawn, rng, least, high):
    longest = drawn.shape.index(max(drawn.shape))
    spots = []
    for shift in (0, 1):
        where = [jax.random.randint(jax.random.fold_in(rng, axis), (), 0, length) for axis, length in enumerate(drawn.shape)]
        where[longest] = (where[longest] + shift) % drawn.shape[longest]
        spots.append(tuple(where))
    return drawn.at[spots[0]].set(least).at[spots[1]].set(high)


def setup_inputs(seed: int = 0, part: int = 0) -> dict:
    key_of = jax.random.split(jax.random.key(seed), 12)
    part_keys = jax.random.split(jax.random.fold_in(key_of[11], part), 12)
    electric = draw_electric(jax.random.fold_in(jax.random.fold_in(key_of[11], part), 71), part)
    magnetic = draw_magnetic(jax.random.fold_in(jax.random.fold_in(key_of[11], part), 71), part)
    polarize = draw_polarize(jax.random.fold_in(jax.random.fold_in(key_of[11], part), 71), part)
    currents = draw_currents(jax.random.fold_in(jax.random.fold_in(key_of[11], part), 71), part)
    material = with_ends(jax.random.randint(key_of[4], (NX, NY, NZ), 0, MATS), jax.random.fold_in(key_of[4], 1), 0, MATS - 1).astype(jnp.int32)
    pole_of = with_ends(jax.random.randint(key_of[5], (MATS,), 0, POLES), jax.random.fold_in(key_of[5], 1), 0, POLES - 1).astype(jnp.int32)
    eps_inf = jnp.clip(jax.random.uniform(key_of[6], (MATS,), jnp.float32, 1.0, 1.2), 1.0, 1.2)
    pole_decay = jnp.clip(jax.random.uniform(key_of[7], (POLES,), jnp.float32, 0.5, 0.95), 0.5, 0.95)
    pole_freq = jnp.clip(jax.random.uniform(key_of[8], (POLES,), jnp.float32, 0.05, 0.2), 0.05, 0.2)
    pole_strength = jnp.clip(jnp.exp(jax.random.uniform(key_of[9], (POLES,), jnp.float32, math.log(0.3), math.log(2.0))), 0.3, 2.0)
    bloch = jnp.clip(jax.random.uniform(part_keys[10], (2,), jnp.float32, -3.140625, 3.140625), -3.140625, 3.140625)
    return dict(electric=electric, magnetic=magnetic, polarize=polarize, currents=currents, material=material, pole_of=pole_of, eps_inf=eps_inf, pole_decay=pole_decay, pole_freq=pole_freq, pole_strength=pole_strength, bloch=bloch)


courant = 0.5

def next_bloch(field, axis, cos_v, sin_v):
    count = field.shape[axis]
    head = lax.slice_in_dim(field, 1, count, axis=axis)
    first = lax.slice_in_dim(field, 0, 1, axis=axis)
    wrapped = jnp.stack([cos_v * first[0] - sin_v * first[1], sin_v * first[0] + cos_v * first[1]])
    return jnp.concatenate([head, wrapped], axis=axis)

def prev_bloch(field, axis, cos_v, sin_v):
    count = field.shape[axis]
    tail = lax.slice_in_dim(field, 0, count - 1, axis=axis)
    last = lax.slice_in_dim(field, count - 1, count, axis=axis)
    wrapped = jnp.stack([cos_v * last[0] + sin_v * last[1], cos_v * last[1] - sin_v * last[0]])
    return jnp.concatenate([wrapped, tail], axis=axis)

def next_z(field):
    return jnp.concatenate([field[..., 1:], jnp.zeros_like(field[..., :1])], axis=-1)

def prev_z(field):
    return jnp.concatenate([jnp.zeros_like(field[..., :1]), field[..., :-1]], axis=-1)

def harmonic_panel(plane, cos_t, sin_t, scale):
    hp = lax.Precision.HIGHEST
    real_a, imag_b = (plane[0], plane[1])
    re_part = (jnp.einsum('xy,my->mx', real_a, cos_t, precision=hp) + jnp.einsum('xy,my->mx', imag_b, sin_t, precision=hp)) * scale
    im_part = (jnp.einsum('xy,my->mx', imag_b, cos_t, precision=hp) - jnp.einsum('xy,my->mx', real_a, sin_t, precision=hp)) * scale
    return jnp.stack([re_part, im_part])

def reference(electric, magnetic, polarize, currents, material, pole_of, eps_inf, pole_decay, pole_freq, pole_strength, bloch):
    cos_x, sin_x = (jnp.cos(bloch[0]), jnp.sin(bloch[0]))
    cos_y, sin_y = (jnp.cos(bloch[1]), jnp.sin(bloch[1]))
    inv_eps = (courant / eps_inf)[material]
    pole_cell = pole_of[material]
    decay = pole_decay[pole_cell]
    freq = pole_freq[pole_cell]
    strength = pole_strength[pole_cell]
    harm_ids = jnp.arange(HARM).astype(jnp.int32)
    ycoords = jnp.arange(NY).astype(jnp.int32)
    angles = 2.0 * math.pi / NY * (harm_ids[:, None] * ycoords[None, :] % NY).astype(jnp.float32)
    cos_t, sin_t = (jnp.cos(angles), jnp.sin(angles))
    scale = 1.0 / math.sqrt(NY)
    e_now, h_now, p_now, j_now = (electric, magnetic, polarize, currents)
    records = []
    for step in range(STEPS):
        ex, ey, ez = (e_now[:, 0], e_now[:, 1], e_now[:, 2])
        curl_e = jnp.stack([next_bloch(ez, 2, cos_y, sin_y) - ez - (next_z(ey) - ey), next_z(ex) - ex - (next_bloch(ez, 1, cos_x, sin_x) - ez), next_bloch(ey, 1, cos_x, sin_x) - ey - (next_bloch(ex, 2, cos_y, sin_y) - ex)], axis=1)
        h_now = h_now - courant * curl_e
        j_now = decay * j_now + freq * (strength * e_now - p_now)
        p_now = p_now + courant * j_now
        hx, hy, hz = (h_now[:, 0], h_now[:, 1], h_now[:, 2])
        curl_h = jnp.stack([hz - prev_bloch(hz, 2, cos_y, sin_y) - (hy - prev_z(hy)), hx - prev_z(hx) - (hz - prev_bloch(hz, 1, cos_x, sin_x)), hy - prev_bloch(hy, 1, cos_x, sin_x) - (hx - prev_bloch(hx, 2, cos_y, sin_y))], axis=1)
        e_now = e_now + inv_eps * (curl_h - j_now)
        records.append(harmonic_panel(e_now[:, 0, :, :, NZ - 1], cos_t, sin_t, scale))
    history = jnp.stack(records, axis=1)
    return (e_now, h_now, p_now, j_now, history)
```

```python
import functools
import math

import jax
import jax.numpy as jnp
import numpy as np
from jax import lax
from jax.experimental import pallas as pl
from jax.experimental.pallas import tpu as pltpu
from jax.sharding import PartitionSpec as P

STEPS = 8
HARM = 8
EDGE = 8
courant = 0.5
VMEM_LIMIT = 24 << 20


def next_y(v):
    return pltpu.roll(v, v.shape[0] - 1, 0)


def prev_y(v):
    return pltpu.roll(v, 1, 0)


def next_z(v):
    lane = lax.broadcasted_iota(jnp.int32, v.shape, 1)
    return jnp.where(lane == v.shape[1] - 1, 0.0, pltpu.roll(v, v.shape[1] - 1, 1))


def prev_z(v):
    lane = lax.broadcasted_iota(jnp.int32, v.shape, 1)
    return jnp.where(lane == 0, 0.0, pltpu.roll(v, 1, 1))


def turn(pair, cos_v, sin_v):
    return cos_v * pair[0] - sin_v * pair[1], sin_v * pair[0] + cos_v * pair[1]


def sublane(v):
    return lax.broadcasted_iota(jnp.int32, v.shape, 0)


def weave(first, second):
    row = sublane(first)
    return jnp.where((row < 2) | (row >= 6), first, pltpu.roll(second, 4, 0))


def edge_rows(ref, at, rows):
    low = ref[at + (slice(0, 8),)]
    high = ref[at + (slice(rows - 8, rows),)]
    return jnp.where(sublane(low) < 4, low, high)


def pack_edges(fields, out, rows):
    e, h, p, j = fields
    parts, comps, planes = e.shape[:3]
    for r in range(parts):
        for g, (one, two) in enumerate(((e, h), (p, j))):
            for k in range(comps):
                for x in range(planes):
                    at = (r, k, x)
                    tile = weave(edge_rows(one, at, rows), edge_rows(two, at, rows))
                    out[((r * 2 + g) * comps + k) * planes + x] = tile


def unpack_edges(recv, fields, phase, rows):
    e, h, p, j = fields
    comps, planes = e.shape[1:3]
    depth = e.shape[4]
    row = lax.broadcasted_iota(jnp.int32, (8, depth), 0)
    cos_v = jnp.where(row < 4, phase[4], phase[6])
    sin_v = jnp.where(row < 4, phase[5], phase[7])
    for g, (one, two) in enumerate(((e, h), (p, j))):
        for k in range(comps):
            for x in range(planes):
                pair = [recv[((r * 2 + g) * comps + k) * planes + x] for r in range(2)]
                for dst in (one, two):
                    re, im = turn(pair, cos_v, sin_v)
                    dst[0, k, x, rows:] = re
                    dst[1, k, x, rows:] = im
                    pair = [pltpu.roll(v, 4, 0) for v in pair]


def curl_e_x(ey, ez):
    return (next_y(ez) - ez) - (next_z(ey) - ey)


def magnetic_full(e, h, r, x, nxt):
    ex, ey, ez = (e[r, k, x] for k in range(3))
    ny_, nz_ = nxt
    h[r, 0, x] = h[r, 0, x] - courant * curl_e_x(ey, ez)
    h[r, 1, x] = h[r, 1, x] - courant * ((next_z(ex) - ex) - (nz_ - ez))
    h[r, 2, x] = h[r, 2, x] - courant * ((ny_ - ey) - (next_y(ex) - ex))


def magnetic_open(ex, ey, ez, hy, hz):
    hy = hy - courant * ((next_z(ex) - ex) + ez)
    hz = hz - courant * ((0.0 - ey) - (next_y(ex) - ex))
    return hy, hz


def polarize_step(e, p, j, coef, r, x):
    for k in range(3):
        now = coef[1, x] * j[r, k, x] + coef[2, x] * (coef[3, x] * e[r, k, x] - p[r, k, x])
        j[r, k, x] = now
        p[r, k, x] = p[r, k, x] + courant * now


def electric_step(e, h, j, coef, r, x, prev):
    hx, hy, hz = (h[r, k, x] for k in range(3))
    inv = coef[0, x]
    e[r, 0, x] = e[r, 0, x] + inv * ((hz - prev_y(hz)) - (hy - prev_z(hy)) - j[r, 0, x])
    dz, dy = hz, hy
    if prev is not None:
        dz, dy = hz - prev[1], hy - prev[0]
    e[r, 1, x] = e[r, 1, x] + inv * ((hx - prev_z(hx)) - dz - j[r, 1, x])
    e[r, 2, x] = e[r, 2, x] + inv * (dy - (hx - prev_y(hx)) - j[r, 2, x])


def response(inv, dhy, dhz):
    dex = inv * ((dhz - prev_y(dhz)) - (dhy - prev_z(dhy)))
    return dex, 0.0 - inv * dhz, inv * dhy


def note_top(e, rec, r, x, step, rows):
    depth = e.shape[4]
    top = e[r, 0, x, 0:rows, depth - 128 :]
    lane = lax.broadcasted_iota(jnp.int32, top.shape, 1)
    rec[r, x] = jnp.where(lane == step, pltpu.roll(top, (step + 1) % 128, 1), rec[r, x])


def start_body(rows, e_in, h_in, p_in, j_in, mat, e, h, p, j, edges):
    for src, dst in ((e_in, e), (h_in, h), (p_in, p), (j_in, j)):
        dst[:, :, :, 0:rows] = src[...]
        dst[:, :, :, rows:] = jnp.zeros(dst.shape[:3] + (EDGE, dst.shape[4]), jnp.float32)
    pack_edges((e_in, h_in, p_in, j_in), edges, rows)
    base = 2 * 2 * 3 * e_in.shape[2]
    for x in range(e_in.shape[2]):
        edges[base + x] = edge_rows(mat, (x,), rows).astype(jnp.float32)


def cell_tables(kind, pole_of, eps, dec, frq, stg):
    vals = [jnp.full(kind.shape, t, jnp.float32) for t in (eps[0], dec[pole_of[0]], frq[pole_of[0]], stg[pole_of[0]])]
    for m in range(1, eps.shape[0]):
        hit = kind == m
        pole = pole_of[m]
        for i, t in enumerate((eps[m], dec[pole], frq[pole], stg[pole])):
            vals[i] = jnp.where(hit, t, vals[i])
    vals[0] = courant / vals[0]
    return vals


def coef_body(rows, mat, pole_of, eps, dec, frq, stg, coef):
    for x in range(mat.shape[0]):
        for y in range(0, rows, 8):
            vals = cell_tables(mat[x, y : y + 8], pole_of, eps, dec, frq, stg)
            for i in range(4):
                coef[i, x, y : y + 8] = vals[i]
        for i in range(4):
            coef[i, x, rows:] = jnp.zeros((EDGE, coef.shape[3]), jnp.float32)


def send_body(rows, first, refs):
    refs = list(refs)
    phase, par, edges = refs[0:3]
    refs = refs[3:]
    if first:
        pole_of, eps, dec, frq, stg = refs[0:5]
        refs = refs[5:]
    e, h, p, j, coef, e0, ev, od, msg = refs[5:]
    planes = e.shape[2]
    last = planes - 1
    unpack_edges(edges, (e, h, p, j), phase, rows)
    if first:
        base = 2 * 2 * 3 * planes
        for x in range(planes):
            kind = edges[base + x].astype(jnp.int32)
            vals = cell_tables(kind, pole_of, eps, dec, frq, stg)
            for i in range(4):
                coef[i, x, rows:] = vals[i]
    up, dn = par[0], 1 - par[0]
    half = 4 * rows
    for r in range(2):
        tiles_d, tiles_u = [], []
        magnetic_full(e, h, r, 0, (e[r, 1, 1], e[r, 2, 1]))
        magnetic_full(e, h, r, last - 1, (e[r, 1, last], e[r, 2, last]))
        ex, ey, ez = (e[r, k, last] for k in range(3))
        h[r, 0, last] = h[r, 0, last] - courant * curl_e_x(ey, ez)
        hs = magnetic_open(ex, ey, ez, h[r, 1, last], h[r, 2, last])
        for k in range(2):
            h[r, 1 + k, last] = hs[k]
            msg[up, (2 * r + k) * rows : (2 * r + k + 1) * rows] = hs[k][0:rows]
            tiles_u.append(hs[k][rows:])
            now = e[r, 1 + k, 0]
            e0[r, k] = now
            msg[dn, (2 * r + k) * rows : (2 * r + k + 1) * rows] = now[0:rows]
            tiles_d.append(now[rows:])
        polarize_step(e, p, j, coef, r, 0)
        polarize_step(e, p, j, coef, r, last)
        electric_step(e, h, j, coef, r, 0, None)
        electric_step(e, h, j, coef, r, last, (h[r, 1, last - 1], h[r, 2, last - 1]))
        ex, ey, ez = (e[r, k, last] for k in range(3))
        hs = magnetic_open(ex, ey, ez, h[r, 1, last], h[r, 2, last])
        for k in range(2):
            at = half + (2 * r + k) * rows
            msg[up, at : at + rows] = hs[k][0:rows]
            now = e[r, 1 + k, 0]
            msg[dn, at : at + rows] = now[0:rows]
            row = sublane(tiles_d[k])
            tiles_d[k] = jnp.where(row == 1, pltpu.roll(now[rows:], 2, 0), tiles_d[k])
        at = 2 * half + 8 * r
        msg[up, at : at + 8] = weave(*tiles_u)
        msg[dn, at : at + 8] = weave(*tiles_d)
    if first:
        at = 2 * half + 16
        msg[up, at : at + rows + EDGE] = coef[0, last]
        msg[dn, at : at + rows + EDGE] = coef[0, 0]
    ev[...] = msg[0]
    od[...] = msg[1]


def inner_body(rows, step, refs):
    e, h, p, j, coef, rec = refs[6:]
    planes = e.shape[2]
    for r in range(2):
        for x in range(1, planes - 2):
            magnetic_full(e, h, r, x, (e[r, 1, x + 1], e[r, 2, x + 1]))
        for x in range(1, planes - 1):
            polarize_step(e, p, j, coef, r, x)
            electric_step(e, h, j, coef, r, x, (h[r, 1, x - 1], h[r, 2, x - 1]))
        for x in range(planes - 1):
            note_top(e, rec, r, x, step, rows)
        for x in range(1, planes - 2):
            magnetic_full(e, h, r, x, (e[r, 1, x + 1], e[r, 2, x + 1]))
        for x in range(1, planes - 1):
            polarize_step(e, p, j, coef, r, x)


def finish_body(rows, step, first, final, refs):
    refs = list(refs)
    phase, par, ev, od, e0 = refs[0:5]
    refs = refs[5:]
    if not first:
        far_in = refs[0]
        refs = refs[1:]
    refs = refs[6:]
    e, h, p, j, rec = refs[0:5]
    coef = refs[5]
    refs = refs[6:]
    if first:
        far = refs[0]
        refs = refs[1:]
    else:
        far = far_in
    if final:
        e_out, h_out, p_out, j_out, wave, harm = refs[0:6]
        refs = refs[6:]
    else:
        edges = refs[0]
        refs = refs[1:]
    msg, = refs
    planes = e.shape[2]
    last = planes - 1
    half = 4 * rows
    msg[0] = ev[...]
    msg[1] = od[...]
    fa, fb = par[0], 1 - par[0]
    if first:
        far[0] = msg[fb, 2 * half + 16 : 2 * half + 16 + rows + EDGE]
        far[1] = msg[fa, 2 * half + 16 : 2 * half + 16 + rows + EDGE]
    inv_lo, inv_hi = far[0], far[1]

    def arrived(side, cos_v, sin_v):
        res = []
        for k in range(2):
            raw = []
            for r in range(2):
                tile = msg[side, 2 * half + 8 * r : 2 * half + 8 * r + 8]
                if k == 1:
                    tile = pltpu.roll(tile, 4, 0)
                at = (2 * r + k) * rows
                one = jnp.concatenate([msg[side, at : at + rows], tile], axis=0)
                two = jnp.concatenate([msg[side, half + at : half + at + rows], pltpu.roll(tile, 6, 0)], axis=0)
                raw.append((one, two))
            res.append((turn((raw[0][0], raw[1][0]), cos_v, sin_v), turn((raw[0][1], raw[1][1]), cos_v, sin_v)))
        return res

    above = arrived(fa, phase[0], phase[1])
    for r in range(2):
        a0y, a0z = above[0][0][r], above[1][0][r]
        dhy, dhz = courant * a0z, 0.0 - courant * a0y
        hy = h[r, 1, last] + dhy
        hz = h[r, 2, last] + dhz
        h[r, 1, last] = hy
        h[r, 2, last] = hz
        for k, d in enumerate(response(coef[0, last], dhy, dhz)):
            e[r, k, last] = e[r, k, last] + d
        note_top(e, rec, r, last, step, rows)
        a1y = above[0][1][r] + inv_hi * hz
        a1z = above[1][1][r] - inv_hi * hy
        magnetic_full(e, h, r, last - 1, (e[r, 1, last], e[r, 2, last]))
        magnetic_full(e, h, r, last, (a1y, a1z))
        polarize_step(e, p, j, coef, r, last)
    below = arrived(fb, phase[2], phase[3])
    for r in range(2):
        dhy, dhz = courant * e0[r, 1], 0.0 - courant * e0[r, 0]
        e[r, 1, 0] = e[r, 1, 0] + coef[0, 0] * (below[1][0][r] + dhz)
        e[r, 2, 0] = e[r, 2, 0] - coef[0, 0] * (below[0][0][r] + dhy)
        dex, dey, dez = response(inv_lo, dhy, dhz)
        hy, hz = magnetic_open(dex, dey, dez, dhy, dhz)
        b1y = below[0][1][r] + hy + courant * e[r, 2, 0]
        b1z = below[1][1][r] + hz - courant * e[r, 1, 0]
        magnetic_full(e, h, r, 0, (e[r, 1, 1], e[r, 2, 1]))
        polarize_step(e, p, j, coef, r, 0)
        electric_step(e, h, j, coef, r, 0, (b1y, b1z))
        for x in range(1, planes):
            electric_step(e, h, j, coef, r, x, (h[r, 1, x - 1], h[r, 2, x - 1]))
        for x in range(planes):
            note_top(e, rec, r, x, step + 1, rows)
    if not final:
        pack_edges((e, h, p, j), edges, rows)
        return
    for src, dst in ((e, e_out), (h, h_out), (p, p_out), (j, j_out)):
        dst[...] = src[:, :, :, 0:rows]
    for x in range(planes):
        re, im = (
            jnp.dot(wave[...], rec[r, x], precision=lax.Precision.HIGHEST, preferred_element_type=jnp.float32)
            for r in range(2)
        )
        harm[0, x] = re[0:HARM] + im[HARM:]
        harm[1, x] = im[0:HARM] - re[HARM:]


def call(body, ins, outs, aliases=None, smem=(), scratch=()):
    shapes = [jax.ShapeDtypeStruct(s, d) for s, d in outs]
    vm = pl.BlockSpec(memory_space=pltpu.VMEM)
    sm = pl.BlockSpec(memory_space=pltpu.SMEM)
    return pl.pallas_call(
        body,
        out_shape=shapes,
        in_specs=[sm if i in smem else vm for i in range(len(ins))],
        out_specs=[vm] * len(outs),
        input_output_aliases=aliases or {},
        scratch_shapes=list(scratch),
        compiler_params=pltpu.CompilerParams(vmem_limit_bytes=VMEM_LIMIT),
    )(*ins)


def swap(block, axis, shift):
    count = lax.axis_size(axis)
    pairs = [(i % count, (i + 1) % count) for i in range(shift, count, 2)]
    return lax.ppermute(block, axis, [q for a, b in pairs for q in ((a, b), (b, a))])


def per_device(
    electric, magnetic, polarize, currents, material, pole_of, eps_inf, pole_decay, pole_freq, pole_strength, bloch
):
    parts, comps, planes, rows, depth = electric.shape
    count_x, count_y = lax.axis_size("gx"), lax.axis_size("gy")
    assert count_x % 2 == 0 and count_y == 2 and planes >= 4
    where_x, where_y = lax.axis_index("gx"), lax.axis_index("gy")
    width_y = rows * count_y
    f32 = jnp.float32
    ext = (rows + EDGE, depth)
    cos_b, sin_b = jnp.cos(bloch), jnp.sin(bloch)

    def hop(at, edge, axis, sign):
        return [jnp.where(at == edge, cos_b[axis], 1.0), jnp.where(at == edge, sign * sin_b[axis], 0.0)]

    phase = jnp.stack(
        hop(where_x, count_x - 1, 0, 1.0)
        + hop(where_x, 0, 0, -1.0)
        + hop(where_y, count_y - 1, 1, 1.0)
        + hop(where_y, 0, 1, -1.0)
    )
    par = jnp.reshape(where_x % 2, (1,)).astype(jnp.int32)
    angle = 2.0 * math.pi / width_y * (np.arange(HARM)[:, None] * np.arange(width_y)[None, :] % width_y)
    waves = np.concatenate([np.cos(angle), np.sin(angle)]) / math.sqrt(width_y)
    waves = np.stack(np.split(waves, count_y, axis=1)).astype(np.float32)
    wave = lax.dynamic_index_in_dim(jnp.asarray(waves), where_y, 0, keepdims=False)

    state_shape = ((parts, comps, planes) + ext, f32)
    coef_shape = ((4, planes) + ext, f32)
    tiles = 2 * 2 * comps * planes
    e, h, p, j, edges = call(
        functools.partial(start_body, rows),
        (electric, magnetic, polarize, currents, material),
        [state_shape] * 4 + [((tiles + planes, 8, depth), f32)],
    )
    tables = (pole_of, eps_inf, pole_decay, pole_freq, pole_strength)
    (coef,) = call(
        functools.partial(coef_body, rows), (material,) + tables, [coef_shape], smem=range(1, 6)
    )
    rec = jnp.zeros((2, planes, rows, 128), f32)
    far = None
    for step in range(0, STEPS, 2):
        first, final = step == 0, step == STEPS - 2
        edges = swap(edges, "gy", 0)
        size = 8 * rows + 16 + (rows + EDGE if first else 0)
        extra = tables if first else ()
        ins = (phase, par, edges) + extra + (e, h, p, j, coef)
        n = 3 + len(extra)
        e, h, p, j, coef, e0, ev, od = call(
            lambda *refs, first=first: send_body(rows, first, refs),
            ins,
            [state_shape] * 4 + [coef_shape, ((2, 2) + ext, f32)] + [((size, depth), f32)] * 2,
            {n + i: i for i in range(5)},
            smem=(0, 1) + tuple(range(3, n)),
            scratch=[pltpu.VMEM((2, size, depth), f32)],
        )
        ev, od = swap(ev, "gx", 0), swap(od, "gx", 1)
        e, h, p, j, coef, rec = call(
            lambda *refs, step=step: inner_body(rows, step, refs),
            (e, h, p, j, coef, rec),
            [state_shape] * 4 + [coef_shape, (rec.shape, f32)],
            {i: i for i in range(6)},
        )
        ins = (phase, par, ev, od, e0) + (() if first else (far,))
        n = len(ins)
        ins = ins + (e, h, p, j, rec, coef)
        outs = [state_shape] * 4 + [(rec.shape, f32), coef_shape]
        if first:
            outs.append(((2,) + ext, f32))
        if final:
            ins = ins + (wave,)
            outs += [(electric.shape, f32)] * 4 + [((2, planes, HARM, 128), f32)]
        else:
            outs.append(((tiles, 8, depth), f32))

        def body(*refs, first=first, final=final, step=step, n=n):
            refs = list(refs)
            if final:
                w = refs.pop(n + 6)
                refs.insert(len(refs) - 2, w)
            finish_body(rows, step, first, final, refs)

        res = call(
            body, ins, outs, {n + i: i for i in range(6)}, smem=(0, 1), scratch=[pltpu.VMEM((2, size, depth), f32)]
        )
        e, h, p, j, rec, coef = res[0:6]
        res = res[6:]
        if first:
            far = res[0]
            res = res[1:]
        if not final:
            edges = res[0]
    *fields, harm = res
    harm = harm + swap(harm, "gy", 0)
    history = jnp.transpose(harm[..., :STEPS], (0, 3, 2, 1))
    return (*fields, history)


def solution(mesh):
    field = P("angle", None, "gx", "gy", None)
    in_specs = (field,) * 4 + (P("gx", "gy", None),) + (P(),) * 5 + (P("angle"),)
    out_specs = (field,) * 4 + (P("angle", None, None, "gx"),)
    return jax.shard_map(per_device, mesh=mesh, in_specs=in_specs, out_specs=out_specs, check_vma=False)
```

```python
import functools
import math

import jax
import jax.numpy as jnp
import numpy as np
from jax import lax
from jax.experimental import pallas as pl
from jax.experimental.pallas import tpu as pltpu
from jax.sharding import PartitionSpec as P

STEPS = 8
HARM = 8
EDGE = 8
courant = 0.5
VMEM_LIMIT = 8 << 20


def next_y(v):
    return pltpu.roll(v, v.shape[0] - 1, 0)


def prev_y(v):
    return pltpu.roll(v, 1, 0)


def next_z(v):
    lane = lax.broadcasted_iota(jnp.int32, v.shape, 1)
    return jnp.where(lane == v.shape[1] - 1, 0.0, pltpu.roll(v, v.shape[1] - 1, 1))


def prev_z(v):
    lane = lax.broadcasted_iota(jnp.int32, v.shape, 1)
    return jnp.where(lane == 0, 0.0, pltpu.roll(v, 1, 1))


def turn(pair, cos_v, sin_v):
    return cos_v * pair[0] - sin_v * pair[1], sin_v * pair[0] + cos_v * pair[1]


def sublane(v):
    return lax.broadcasted_iota(jnp.int32, v.shape, 0)


def weave(first, second):
    row = sublane(first)
    return jnp.where((row < 2) | (row >= 6), first, pltpu.roll(second, 4, 0))


def edge_rows(ref, at, rows):
    low = ref[at + (slice(0, 8),)]
    high = ref[at + (slice(rows - 8, rows),)]
    return jnp.where(sublane(low) < 4, low, high)


def pack_edges(fields, out, rows):
    e, h, p, j = fields
    parts, comps, planes = e.shape[:3]
    for r in range(parts):
        for g, (one, two) in enumerate(((e, h), (p, j))):
            for k in range(comps):
                for x in range(planes):
                    at = (r, k, x)
                    tile = weave(edge_rows(one, at, rows), edge_rows(two, at, rows))
                    out[((r * 2 + g) * comps + k) * planes + x] = tile


def wrap_phase(cs, axis, name, up):
    at, count = lax.axis_index(name), lax.axis_size(name)
    wraps = at == (count - 1 if up else 0)
    sine = cs[2 + axis, 0:1]
    return jnp.where(wraps, cs[axis, 0:1], 1.0), jnp.where(wraps, sine if up else 0.0 - sine, 0.0)


def unpack_edges(recv, fields, cs, rows):
    e, h, p, j = fields
    up, dn = wrap_phase(cs, 1, "gy", True), wrap_phase(cs, 1, "gy", False)
    comps, planes = e.shape[1:3]
    depth = e.shape[4]
    row = lax.broadcasted_iota(jnp.int32, (8, depth), 0)
    cos_v = jnp.where(row < 4, up[0], dn[0])
    sin_v = jnp.where(row < 4, up[1], dn[1])
    for g, (one, two) in enumerate(((e, h), (p, j))):
        for k in range(comps):
            for x in range(planes):
                pair = [recv[((r * 2 + g) * comps + k) * planes + x] for r in range(2)]
                for dst in (one, two):
                    re, im = turn(pair, cos_v, sin_v)
                    dst[0, k, x, rows:] = re
                    dst[1, k, x, rows:] = im
                    pair = [pltpu.roll(v, 4, 0) for v in pair]


def curl_e_x(ey, ez):
    return (next_y(ez) - ez) - (next_z(ey) - ey)


def magnetic_full(e, h, r, x, nxt):
    ex, ey, ez = (e[r, k, x] for k in range(3))
    ny_, nz_ = nxt
    h[r, 0, x] = h[r, 0, x] - courant * curl_e_x(ey, ez)
    h[r, 1, x] = h[r, 1, x] - courant * ((next_z(ex) - ex) - (nz_ - ez))
    h[r, 2, x] = h[r, 2, x] - courant * ((ny_ - ey) - (next_y(ex) - ex))


def magnetic_open(ex, ey, ez, hy, hz):
    hy = hy - courant * ((next_z(ex) - ex) + ez)
    hz = hz - courant * ((0.0 - ey) - (next_y(ex) - ex))
    return hy, hz


def polarize_step(e, p, j, coef, r, x):
    for k in range(3):
        now = coef[1, x] * j[r, k, x] + coef[2, x] * (coef[3, x] * e[r, k, x] - p[r, k, x])
        j[r, k, x] = now
        p[r, k, x] = p[r, k, x] + courant * now


def electric_step(e, h, j, coef, r, x, prev):
    hx, hy, hz = (h[r, k, x] for k in range(3))
    inv = coef[0, x]
    e[r, 0, x] = e[r, 0, x] + inv * ((hz - prev_y(hz)) - (hy - prev_z(hy)) - j[r, 0, x])
    dz, dy = hz, hy
    if prev is not None:
        dz, dy = hz - prev[1], hy - prev[0]
    e[r, 1, x] = e[r, 1, x] + inv * ((hx - prev_z(hx)) - dz - j[r, 1, x])
    e[r, 2, x] = e[r, 2, x] + inv * (dy - (hx - prev_y(hx)) - j[r, 2, x])


def response(inv, dhy, dhz):
    dex = inv * ((dhz - prev_y(dhz)) - (dhy - prev_z(dhy)))
    return dex, 0.0 - inv * dhz, inv * dhy


def note_top(e, rec, r, x, step, rows):
    depth = e.shape[4]
    top = e[r, 0, x, 0:rows, depth - 128 :]
    lane = lax.broadcasted_iota(jnp.int32, top.shape, 1)
    rec[r, x] = jnp.where(lane == step, pltpu.roll(top, (step + 1) % 128, 1), rec[r, x])


def start_body(rows, e_in, h_in, p_in, j_in, mat_in, e, h, p, j, mat, edges, sems):
    pairs = [(src, dst.at[:, :, :, 0:rows]) for src, dst in ((e_in, e), (h_in, h), (p_in, p), (j_in, j))]
    copies = [pltpu.make_async_copy(src, dst, sems.at[i]) for i, (src, dst) in enumerate(pairs + [(mat_in, mat)])]
    for c in copies:
        c.start()
    for dst in (e, h, p, j):
        dst[:, :, :, rows:] = jnp.zeros(dst.shape[:3] + (EDGE, dst.shape[4]), jnp.float32)
    for c in copies:
        c.wait()
    pack_edges((e, h, p, j), edges, rows)
    base = 2 * 2 * 3 * e.shape[2]
    for x in range(e.shape[2]):
        edges[base + x] = edge_rows(mat, (x,), rows).astype(jnp.float32)


def store_body(rows, e, h, p, j, e_out, h_out, p_out, j_out, sems):
    pairs = ((e, e_out), (h, h_out), (p, p_out), (j, j_out))
    copies = [
        pltpu.make_async_copy(src.at[:, :, :, 0:rows], dst, sems.at[i]) for i, (src, dst) in enumerate(pairs)
    ]
    for c in copies:
        c.start()
    for c in copies:
        c.wait()


def panel_body(own, other, out):
    for r in range(2):
        for x in range(own.shape[1]):
            out[r, :, x] = jnp.transpose(own[r, x] + other[r, x])[0:STEPS]


def cell_tables(kind, pole_of, eps, dec, frq, stg):
    vals = [jnp.full(kind.shape, t, jnp.float32) for t in (eps[0], dec[pole_of[0]], frq[pole_of[0]], stg[pole_of[0]])]
    for m in range(1, eps.shape[0]):
        hit = kind == m
        pole = pole_of[m]
        for i, t in enumerate((eps[m], dec[pole], frq[pole], stg[pole])):
            vals[i] = jnp.where(hit, t, vals[i])
    vals[0] = courant / vals[0]
    return vals


def coef_body(rows, mat, pole_of, eps, dec, frq, stg, bloch, coef, cs, rec):
    rec[...] = jnp.zeros(rec.shape, jnp.float32)
    for i in range(2):
        turns = jnp.full(cs.shape[1:], bloch[i], jnp.float32)
        cs[i] = jnp.cos(turns)
        cs[2 + i] = jnp.sin(turns)
    for x in range(mat.shape[0]):
        for y in range(0, rows, 8):
            vals = cell_tables(mat[x, y : y + 8], pole_of, eps, dec, frq, stg)
            for i in range(4):
                coef[i, x, y : y + 8] = vals[i]
        for i in range(4):
            coef[i, x, rows:] = jnp.zeros((EDGE, coef.shape[3]), jnp.float32)


def send_body(rows, first, refs):
    refs = list(refs)
    cs, edges = refs[0:2]
    refs = refs[2:]
    if first:
        pole_of, eps, dec, frq, stg = refs[0:5]
        refs = refs[5:]
    e, h, p, j, coef, e0, ev, od, msg = refs[5:]
    planes = e.shape[2]
    last = planes - 1
    unpack_edges(edges, (e, h, p, j), cs, rows)
    if first:
        base = 2 * 2 * 3 * planes
        for x in range(planes):
            kind = edges[base + x].astype(jnp.int32)
            vals = cell_tables(kind, pole_of, eps, dec, frq, stg)
            for i in range(4):
                coef[i, x, rows:] = vals[i]
    up = lax.axis_index("gx") % 2
    dn = 1 - up
    half = 4 * rows
    for r in range(2):
        tiles_d, tiles_u = [], []
        magnetic_full(e, h, r, 0, (e[r, 1, 1], e[r, 2, 1]))
        magnetic_full(e, h, r, last - 1, (e[r, 1, last], e[r, 2, last]))
        ex, ey, ez = (e[r, k, last] for k in range(3))
        h[r, 0, last] = h[r, 0, last] - courant * curl_e_x(ey, ez)
        hs = magnetic_open(ex, ey, ez, h[r, 1, last], h[r, 2, last])
        for k in range(2):
            h[r, 1 + k, last] = hs[k]
            msg[up, (2 * r + k) * rows : (2 * r + k + 1) * rows] = hs[k][0:rows]
            tiles_u.append(hs[k][rows:])
            now = e[r, 1 + k, 0]
            e0[r, k] = now
            msg[dn, (2 * r + k) * rows : (2 * r + k + 1) * rows] = now[0:rows]
            tiles_d.append(now[rows:])
        polarize_step(e, p, j, coef, r, 0)
        polarize_step(e, p, j, coef, r, last)
        electric_step(e, h, j, coef, r, 0, None)
        electric_step(e, h, j, coef, r, last, (h[r, 1, last - 1], h[r, 2, last - 1]))
        ex, ey, ez = (e[r, k, last] for k in range(3))
        hs = magnetic_open(ex, ey, ez, h[r, 1, last], h[r, 2, last])
        for k in range(2):
            at = half + (2 * r + k) * rows
            msg[up, at : at + rows] = hs[k][0:rows]
            now = e[r, 1 + k, 0]
            msg[dn, at : at + rows] = now[0:rows]
            row = sublane(tiles_d[k])
            tiles_d[k] = jnp.where(row == 1, pltpu.roll(now[rows:], 2, 0), tiles_d[k])
        at = 2 * half + 8 * r
        msg[up, at : at + 8] = weave(*tiles_u)
        msg[dn, at : at + 8] = weave(*tiles_d)
    if first:
        at = 2 * half + 16
        msg[up, at : at + rows + EDGE] = coef[0, last]
        msg[dn, at : at + rows + EDGE] = coef[0, 0]
    ev[...] = msg[0]
    od[...] = msg[1]


def inner_body(rows, step, refs):
    e, h, p, j, coef, rec = refs[6:]
    planes = e.shape[2]
    for r in range(2):
        for x in range(1, planes - 2):
            magnetic_full(e, h, r, x, (e[r, 1, x + 1], e[r, 2, x + 1]))
        for x in range(1, planes - 1):
            polarize_step(e, p, j, coef, r, x)
            electric_step(e, h, j, coef, r, x, (h[r, 1, x - 1], h[r, 2, x - 1]))
        for x in range(planes - 1):
            note_top(e, rec, r, x, step, rows)
        for x in range(1, planes - 2):
            magnetic_full(e, h, r, x, (e[r, 1, x + 1], e[r, 2, x + 1]))
        for x in range(1, planes - 1):
            polarize_step(e, p, j, coef, r, x)


def finish_body(rows, step, first, final, refs):
    refs = list(refs)
    cs, ev, od, e0 = refs[0:4]
    refs = refs[4:]
    if not first:
        far_in = refs[0]
        refs = refs[1:]
    refs = refs[6:]
    e, h, p, j, rec = refs[0:5]
    coef = refs[5]
    refs = refs[6:]
    if first:
        far = refs[0]
        refs = refs[1:]
    else:
        far = far_in
    if final:
        waves, harm = refs[0:2]
        refs = refs[2:]
    else:
        edges = refs[0]
        refs = refs[1:]
    msg, = refs
    planes = e.shape[2]
    last = planes - 1
    half = 4 * rows
    msg[0] = ev[...]
    msg[1] = od[...]
    fa = lax.axis_index("gx") % 2
    fb = 1 - fa
    if first:
        far[0] = msg[fb, 2 * half + 16 : 2 * half + 16 + rows + EDGE]
        far[1] = msg[fa, 2 * half + 16 : 2 * half + 16 + rows + EDGE]
    inv_lo, inv_hi = far[0], far[1]

    def arrived(side, cos_v, sin_v):
        res = []
        for k in range(2):
            raw = []
            for r in range(2):
                tile = msg[side, 2 * half + 8 * r : 2 * half + 8 * r + 8]
                if k == 1:
                    tile = pltpu.roll(tile, 4, 0)
                at = (2 * r + k) * rows
                one = jnp.concatenate([msg[side, at : at + rows], tile], axis=0)
                two = jnp.concatenate([msg[side, half + at : half + at + rows], pltpu.roll(tile, 6, 0)], axis=0)
                raw.append((one, two))
            res.append((turn((raw[0][0], raw[1][0]), cos_v, sin_v), turn((raw[0][1], raw[1][1]), cos_v, sin_v)))
        return res

    above = arrived(fa, *wrap_phase(cs, 0, "gx", True))
    for r in range(2):
        a0y, a0z = above[0][0][r], above[1][0][r]
        dhy, dhz = courant * a0z, 0.0 - courant * a0y
        hy = h[r, 1, last] + dhy
        hz = h[r, 2, last] + dhz
        h[r, 1, last] = hy
        h[r, 2, last] = hz
        for k, d in enumerate(response(coef[0, last], dhy, dhz)):
            e[r, k, last] = e[r, k, last] + d
        note_top(e, rec, r, last, step, rows)
        a1y = above[0][1][r] + inv_hi * hz
        a1z = above[1][1][r] - inv_hi * hy
        magnetic_full(e, h, r, last - 1, (e[r, 1, last], e[r, 2, last]))
        magnetic_full(e, h, r, last, (a1y, a1z))
        polarize_step(e, p, j, coef, r, last)
    below = arrived(fb, *wrap_phase(cs, 0, "gx", False))
    for r in range(2):
        dhy, dhz = courant * e0[r, 1], 0.0 - courant * e0[r, 0]
        e[r, 1, 0] = e[r, 1, 0] + coef[0, 0] * (below[1][0][r] + dhz)
        e[r, 2, 0] = e[r, 2, 0] - coef[0, 0] * (below[0][0][r] + dhy)
        dex, dey, dez = response(inv_lo, dhy, dhz)
        hy, hz = magnetic_open(dex, dey, dez, dhy, dhz)
        b1y = below[0][1][r] + hy + courant * e[r, 2, 0]
        b1z = below[1][1][r] + hz - courant * e[r, 1, 0]
        magnetic_full(e, h, r, 0, (e[r, 1, 1], e[r, 2, 1]))
        polarize_step(e, p, j, coef, r, 0)
        electric_step(e, h, j, coef, r, 0, (b1y, b1z))
        for x in range(1, planes):
            electric_step(e, h, j, coef, r, x, (h[r, 1, x - 1], h[r, 2, x - 1]))
        for x in range(planes):
            note_top(e, rec, r, x, step + 1, rows)
    if not final:
        pack_edges((e, h, p, j), edges, rows)
        return
    wave = waves[lax.axis_index("gy")]
    for x in range(planes):
        re, im = (
            jnp.dot(wave, rec[r, x], precision=lax.Precision.HIGHEST, preferred_element_type=jnp.float32)
            for r in range(2)
        )
        harm[0, x] = re[0:HARM] + im[HARM:]
        harm[1, x] = im[0:HARM] - re[HARM:]


def call(body, ins, outs, aliases=None, smem=(), hbm_in=(), hbm_out=False, scratch=(), cost=0):
    shapes = [jax.ShapeDtypeStruct(s, d) for s, d in outs]
    vm = pl.BlockSpec(memory_space=pltpu.VMEM)
    sm = pl.BlockSpec(memory_space=pltpu.SMEM)
    hbm = pl.BlockSpec(memory_space=pltpu.HBM)
    return pl.pallas_call(
        body,
        out_shape=shapes,
        in_specs=[sm if i in smem else hbm if i in hbm_in else vm for i in range(len(ins))],
        out_specs=[hbm if hbm_out else vm] * len(outs),
        input_output_aliases=aliases or {},
        scratch_shapes=list(scratch),
        cost_estimate=pl.CostEstimate(flops=cost, bytes_accessed=cost, transcendentals=0),
        compiler_params=pltpu.CompilerParams(vmem_limit_bytes=VMEM_LIMIT),
    )(*ins)


def swap(block, axis, shift):
    count = lax.axis_size(axis)
    pairs = [(i % count, (i + 1) % count) for i in range(shift, count, 2)]
    return lax.ppermute(block, axis, [q for a, b in pairs for q in ((a, b), (b, a))])


def per_device(
    electric, magnetic, polarize, currents, material, pole_of, eps_inf, pole_decay, pole_freq, pole_strength, bloch
):
    parts, comps, planes, rows, depth = electric.shape
    count_x, count_y = lax.axis_size("gx"), lax.axis_size("gy")
    assert count_x % 2 == 0 and count_y == 2 and planes >= 4
    width_y = rows * count_y
    f32 = jnp.float32
    ext = (rows + EDGE, depth)
    angle = 2.0 * math.pi / width_y * (np.arange(HARM)[:, None] * np.arange(width_y)[None, :] % width_y)
    waves = np.concatenate([np.cos(angle), np.sin(angle)]) / math.sqrt(width_y)
    waves = jnp.asarray(np.stack(np.split(waves, count_y, axis=1)).astype(np.float32))

    state_shape = ((parts, comps, planes) + ext, f32)
    coef_shape = ((4, planes) + ext, f32)
    tiles = 2 * 2 * comps * planes
    e, h, p, j, mat, edges = call(
        functools.partial(start_body, rows),
        (electric, magnetic, polarize, currents, material),
        [state_shape] * 4 + [(material.shape, material.dtype), ((tiles + planes, 8, depth), f32)],
        hbm_in=range(5),
        scratch=[pltpu.SemaphoreType.DMA((5,))],
    )
    tables = (pole_of, eps_inf, pole_decay, pole_freq, pole_strength)
    coef, cs, rec = call(
        functools.partial(coef_body, rows),
        (mat,) + tables + (bloch,),
        [coef_shape, ((4, 8, depth), f32), ((2, planes, rows, 128), f32)],
        smem=range(1, 7),
        cost=1 << 20,
    )
    far = None
    for step in range(0, STEPS, 2):
        first, final = step == 0, step == STEPS - 2
        edges = swap(edges, "gy", 0)
        size = 8 * rows + 16 + (rows + EDGE if first else 0)
        extra = tables if first else ()
        ins = (cs, edges) + extra + (e, h, p, j, coef)
        n = 2 + len(extra)
        e, h, p, j, coef, e0, ev, od = call(
            lambda *refs, first=first: send_body(rows, first, refs),
            ins,
            [state_shape] * 4 + [coef_shape, ((2, 2) + ext, f32)] + [((size, depth), f32)] * 2,
            {n + i: i for i in range(5)},
            smem=tuple(range(2, n)),
            scratch=[pltpu.VMEM((2, size, depth), f32)],
        )
        ev, od = swap(ev, "gx", 0), swap(od, "gx", 1)
        e, h, p, j, coef, rec = call(
            lambda *refs, step=step: inner_body(rows, step, refs),
            (e, h, p, j, coef, rec),
            [state_shape] * 4 + [coef_shape, (rec.shape, f32)],
            {i: i for i in range(6)},
            cost=1 << 20,
        )
        ins = (cs, ev, od, e0) + (() if first else (far,))
        n = len(ins)
        ins = ins + (e, h, p, j, rec, coef)
        outs = [state_shape] * 4 + [(rec.shape, f32), coef_shape]
        if first:
            outs.append(((2,) + ext, f32))
        if final:
            ins = ins + (waves,)
            outs.append(((2, planes, HARM, 128), f32))
        else:
            outs.append(((tiles, 8, depth), f32))

        def body(*refs, first=first, final=final, step=step, n=n):
            refs = list(refs)
            if final:
                w = refs.pop(n + 6)
                refs.insert(len(refs) - 2, w)
            finish_body(rows, step, first, final, refs)

        res = call(
            body, ins, outs, {n + i: i for i in range(6)}, scratch=[pltpu.VMEM((2, size, depth), f32)]
        )
        e, h, p, j, rec, coef = res[0:6]
        res = res[6:]
        if first:
            far = res[0]
            res = res[1:]
        if not final:
            edges = res[0]
    (harm,) = res
    other = swap(harm, "gy", 0)
    fields = call(
        functools.partial(store_body, rows),
        (e, h, p, j),
        [(electric.shape, f32)] * 4,
        hbm_out=True,
        scratch=[pltpu.SemaphoreType.DMA((4,))],
        cost=1 << 22,
    )
    (panel,) = call(panel_body, (harm, other), [((2, STEPS, planes, HARM), f32)])
    return (*fields, jnp.transpose(panel, (0, 1, 3, 2)))


def solution(mesh):
    field = P("angle", None, "gx", "gy", None)
    in_specs = (field,) * 4 + (P("gx", "gy", None),) + (P(),) * 5 + (P("angle"),)
    out_specs = (field,) * 4 + (P("angle", None, None, "gx"),)
    return jax.shard_map(per_device, mesh=mesh, in_specs=in_specs, out_specs=out_specs, check_vma=False)
```

```python
import functools
import math

import jax
import jax.numpy as jnp
import numpy as np
from jax import lax
from jax.experimental import pallas as pl
from jax.experimental.pallas import tpu as pltpu
from jax.sharding import PartitionSpec as P

STEPS = 8
HARM = 8
EDGE = 8
ORDER = (0, 1)
courant = 0.5
VMEM_LIMIT = 8 << 20


def next_y(v):
    return pltpu.roll(v, v.shape[0] - 1, 0)


def prev_y(v):
    return pltpu.roll(v, 1, 0)


def next_z(v):
    lane = lax.broadcasted_iota(jnp.int32, v.shape, 1)
    return jnp.where(lane == v.shape[1] - 1, 0.0, pltpu.roll(v, v.shape[1] - 1, 1))


def prev_z(v):
    lane = lax.broadcasted_iota(jnp.int32, v.shape, 1)
    return jnp.where(lane == 0, 0.0, pltpu.roll(v, 1, 1))


def turn(pair, cos_v, sin_v):
    return cos_v * pair[0] - sin_v * pair[1], sin_v * pair[0] + cos_v * pair[1]


def sublane(v):
    return lax.broadcasted_iota(jnp.int32, v.shape, 0)


def weave(first, second):
    row = sublane(first)
    return jnp.where((row < 2) | (row >= 6), first, pltpu.roll(second, 4, 0))


def edge_rows(ref, at, rows):
    low = ref[at + (slice(0, 8),)]
    high = ref[at + (slice(rows - 8, rows),)]
    return jnp.where(sublane(low) < 4, low, high)


def pack_edges(fields, out, rows, xs):
    e, h, p, j = fields
    for r in range(2):
        for g, (one, two) in enumerate(((e, h), (p, j))):
            for k in range(3):
                for i, x in enumerate(xs):
                    at = (r, k, x)
                    tile = weave(edge_rows(one, at, rows), edge_rows(two, at, rows))
                    out[((r * 2 + g) * 3 + k) * len(xs) + i] = tile


def wrap_phase(cs, axis, name, up):
    at, count = lax.axis_index(name), lax.axis_size(name)
    wraps = at == (count - 1 if up else 0)
    sine = cs[2 + axis, 0:1]
    return jnp.where(wraps, cs[axis, 0:1], 1.0), jnp.where(wraps, sine if up else 0.0 - sine, 0.0)


def unpack_edges(recv, fields, cs, rows, xs):
    e, h, p, j = fields
    up, dn = wrap_phase(cs, 1, "gy", True), wrap_phase(cs, 1, "gy", False)
    depth = e.shape[4]
    row = lax.broadcasted_iota(jnp.int32, (8, depth), 0)
    cos_v = jnp.where(row < 4, up[0], dn[0])
    sin_v = jnp.where(row < 4, up[1], dn[1])
    for g, (one, two) in enumerate(((e, h), (p, j))):
        for k in range(3):
            for i, x in enumerate(xs):
                pair = [recv[((r * 2 + g) * 3 + k) * len(xs) + i] for r in range(2)]
                for dst in (one, two):
                    re, im = turn(pair, cos_v, sin_v)
                    dst[0, k, x, rows:] = re
                    dst[1, k, x, rows:] = im
                    pair = [pltpu.roll(v, 4, 0) for v in pair]


def curl_e_x(ey, ez):
    return (next_y(ez) - ez) - (next_z(ey) - ey)


def magnetic_full(e, h, r, x, nxt):
    ex, ey, ez = (e[r, k, x] for k in range(3))
    ny_, nz_ = nxt
    h[r, 0, x] = h[r, 0, x] - courant * curl_e_x(ey, ez)
    h[r, 1, x] = h[r, 1, x] - courant * ((next_z(ex) - ex) - (nz_ - ez))
    h[r, 2, x] = h[r, 2, x] - courant * ((ny_ - ey) - (next_y(ex) - ex))


def magnetic_open(ex, ey, ez, hy, hz):
    hy = hy - courant * ((next_z(ex) - ex) + ez)
    hz = hz - courant * ((0.0 - ey) - (next_y(ex) - ex))
    return hy, hz


def polarize_step(e, p, j, coef, r, x):
    for k in range(3):
        now = coef[1, x] * j[r, k, x] + coef[2, x] * (coef[3, x] * e[r, k, x] - p[r, k, x])
        j[r, k, x] = now
        p[r, k, x] = p[r, k, x] + courant * now


def electric_step(e, h, j, coef, r, x, prev):
    hx, hy, hz = (h[r, k, x] for k in range(3))
    inv = coef[0, x]
    e[r, 0, x] = e[r, 0, x] + inv * ((hz - prev_y(hz)) - (hy - prev_z(hy)) - j[r, 0, x])
    dz, dy = hz, hy
    if prev is not None:
        dz, dy = hz - prev[1], hy - prev[0]
    e[r, 1, x] = e[r, 1, x] + inv * ((hx - prev_z(hx)) - dz - j[r, 1, x])
    e[r, 2, x] = e[r, 2, x] + inv * (dy - (hx - prev_y(hx)) - j[r, 2, x])


def response(inv, dhy, dhz):
    dex = inv * ((dhz - prev_y(dhz)) - (dhy - prev_z(dhy)))
    return dex, 0.0 - inv * dhz, inv * dhy


def note_top(e, rec, r, x, step, rows):
    depth = e.shape[4]
    top = e[r, 0, x, 0:rows, depth - 128 :]
    lane = lax.broadcasted_iota(jnp.int32, top.shape, 1)
    rec[r, x] = jnp.where(lane == step, pltpu.roll(top, (step + 1) % 128, 1), rec[r, x])


def start_body(rows, e_in, h_in, p_in, j_in, mat_in, e, h, p, j, mat, edges, sems):
    pairs = [(src, dst.at[:, :, :, 0:rows]) for src, dst in ((e_in, e), (h_in, h), (p_in, p), (j_in, j))]
    copies = [pltpu.make_async_copy(src, dst, sems.at[i]) for i, (src, dst) in enumerate(pairs + [(mat_in, mat)])]
    for c in copies:
        c.start()
    for dst in (e, h, p, j):
        dst[:, :, :, rows:] = jnp.zeros(dst.shape[:3] + (EDGE, dst.shape[4]), jnp.float32)
    for c in copies:
        c.wait()
    pack_edges((e, h, p, j), edges, rows, range(e.shape[2]))
    base = 2 * 2 * 3 * e.shape[2]
    for x in range(e.shape[2]):
        edges[base + x] = edge_rows(mat, (x,), rows).astype(jnp.float32)


def store_body(rows, e, h, p, j, e_out, h_out, p_out, j_out, sems):
    pairs = ((e, e_out), (h, h_out), (p, p_out), (j, j_out))
    copies = [
        pltpu.make_async_copy(src.at[:, :, :, 0:rows], dst, sems.at[i]) for i, (src, dst) in enumerate(pairs)
    ]
    for c in copies:
        c.start()
    for c in copies:
        c.wait()


def panel_body(own, other, out):
    for r in range(2):
        for x in range(own.shape[1]):
            out[r, :, x] = jnp.transpose(own[r, x] + other[r, x])[0:STEPS]


def cell_tables(kind, pole_of, eps, dec, frq, stg):
    vals = [jnp.full(kind.shape, t, jnp.float32) for t in (eps[0], dec[pole_of[0]], frq[pole_of[0]], stg[pole_of[0]])]
    for m in range(1, eps.shape[0]):
        hit = kind == m
        pole = pole_of[m]
        for i, t in enumerate((eps[m], dec[pole], frq[pole], stg[pole])):
            vals[i] = jnp.where(hit, t, vals[i])
    vals[0] = courant / vals[0]
    return vals


def coef_body(rows, mat, pole_of, eps, dec, frq, stg, bloch, coef, cs, rec):
    rec[...] = jnp.zeros(rec.shape, jnp.float32)
    for i in range(2):
        turns = jnp.full(cs.shape[1:], bloch[i], jnp.float32)
        cs[i] = jnp.cos(turns)
        cs[2 + i] = jnp.sin(turns)
    for x in range(mat.shape[0]):
        for y in range(0, rows, 8):
            vals = cell_tables(mat[x, y : y + 8], pole_of, eps, dec, frq, stg)
            for i in range(4):
                coef[i, x, y : y + 8] = vals[i]
        for i in range(4):
            coef[i, x, rows:] = jnp.zeros((EDGE, coef.shape[3]), jnp.float32)


def by_side(which, upper, lower):
    mine = lax.axis_index("gx") % 2 == which
    pl.when(mine)(upper)
    pl.when(jnp.logical_not(mine))(lower)


def send_body(rows, which, first, step, refs):
    refs = list(refs)
    second = which == ORDER[1]
    if second:
        rec = refs.pop()
        refs.pop(5 if first else 7)
    if first and which == ORDER[0]:
        cs, edges, pole_of, eps, dec, frq, stg = refs[0:7]
        e, h, p, j, coef, e0, out = refs[12:]
    elif first:
        e, h, p, j, e0, out = refs[5:]
        coef = refs[4]
    else:
        cs, edges = refs[0:2]
        coef = refs[6]
        e, h, p, j, e0, out = refs[7:]
    planes = e.shape[2]
    last = planes - 1
    half = 4 * rows
    if first and which == ORDER[0]:
        unpack_edges(edges, (e, h, p, j), cs, rows, range(planes))
        base = 2 * 2 * 3 * planes
        for x in range(planes):
            kind = edges[base + x].astype(jnp.int32)
            vals = cell_tables(kind, pole_of, eps, dec, frq, stg)
            for i in range(4):
                coef[i, x, rows:] = vals[i]

    def upper():
        if not first:
            unpack_edges(edges, (e, h, p, j), cs, rows, (last - 1, last))
        for r in range(2):
            tiles = []
            magnetic_full(e, h, r, last - 1, (e[r, 1, last], e[r, 2, last]))
            ex, ey, ez = (e[r, k, last] for k in range(3))
            h[r, 0, last] = h[r, 0, last] - courant * curl_e_x(ey, ez)
            hs = magnetic_open(ex, ey, ez, h[r, 1, last], h[r, 2, last])
            for k in range(2):
                h[r, 1 + k, last] = hs[k]
                out[(2 * r + k) * rows : (2 * r + k + 1) * rows] = hs[k][0:rows]
                tiles.append(hs[k][rows:])
            polarize_step(e, p, j, coef, r, last)
            electric_step(e, h, j, coef, r, last, (h[r, 1, last - 1], h[r, 2, last - 1]))
            ex, ey, ez = (e[r, k, last] for k in range(3))
            hs = magnetic_open(ex, ey, ez, h[r, 1, last], h[r, 2, last])
            for k in range(2):
                at = half + (2 * r + k) * rows
                out[at : at + rows] = hs[k][0:rows]
            at = 2 * half + 8 * r
            out[at : at + 8] = weave(*tiles)
        if first:
            out[2 * half + 16 :] = coef[0, last]

    def lower():
        if not first:
            unpack_edges(edges, (e, h, p, j), cs, rows, (0, 1))
        for r in range(2):
            tiles = []
            magnetic_full(e, h, r, 0, (e[r, 1, 1], e[r, 2, 1]))
            for k in range(2):
                now = e[r, 1 + k, 0]
                e0[r, k] = now
                out[(2 * r + k) * rows : (2 * r + k + 1) * rows] = now[0:rows]
                tiles.append(now[rows:])
            polarize_step(e, p, j, coef, r, 0)
            electric_step(e, h, j, coef, r, 0, None)
            for k in range(2):
                at = half + (2 * r + k) * rows
                now = e[r, 1 + k, 0]
                out[at : at + rows] = now[0:rows]
                row = sublane(tiles[k])
                tiles[k] = jnp.where(row == 1, pltpu.roll(now[rows:], 2, 0), tiles[k])
            at = 2 * half + 8 * r
            out[at : at + 8] = weave(*tiles)
        if first:
            out[2 * half + 16 :] = coef[0, 0]

    by_side(which, upper, lower)
    if second:
        inner_part(rows, step, (e, h, p, j, rec), coef)


def inner_part(rows, step, state, coef):
    e, h, p, j, rec = state
    planes = e.shape[2]
    for r in range(2):
        for x in range(1, planes - 2):
            magnetic_full(e, h, r, x, (e[r, 1, x + 1], e[r, 2, x + 1]))
        for x in range(1, planes - 1):
            polarize_step(e, p, j, coef, r, x)
            electric_step(e, h, j, coef, r, x, (h[r, 1, x - 1], h[r, 2, x - 1]))
        for x in range(planes - 1):
            note_top(e, rec, r, x, step, rows)
        for x in range(1, planes - 2):
            magnetic_full(e, h, r, x, (e[r, 1, x + 1], e[r, 2, x + 1]))
        for x in range(1, planes - 1):
            polarize_step(e, p, j, coef, r, x)


def finish_body(rows, which, step, final, refs):
    cs, msg, e0, far, coef = refs[0:5]
    refs = refs[10:]
    e, h, p, j, rec = refs[0:5]
    planes = e.shape[2]
    last = planes - 1
    half = 4 * rows
    inv_far = far[2 * half + 16 : 2 * half + 16 + rows + EDGE]

    def arrived(cos_v, sin_v):
        res = []
        for k in range(2):
            raw = []
            for r in range(2):
                tile = msg[2 * half + 8 * r : 2 * half + 8 * r + 8]
                if k == 1:
                    tile = pltpu.roll(tile, 4, 0)
                at = (2 * r + k) * rows
                one = jnp.concatenate([msg[at : at + rows], tile], axis=0)
                two = jnp.concatenate([msg[half + at : half + at + rows], pltpu.roll(tile, 6, 0)], axis=0)
                raw.append((one, two))
            res.append((turn((raw[0][0], raw[1][0]), cos_v, sin_v), turn((raw[0][1], raw[1][1]), cos_v, sin_v)))
        return res

    def upper():
        above = arrived(*wrap_phase(cs, 0, "gx", True))
        for r in range(2):
            a0y, a0z = above[0][0][r], above[1][0][r]
            dhy, dhz = courant * a0z, 0.0 - courant * a0y
            hy = h[r, 1, last] + dhy
            hz = h[r, 2, last] + dhz
            h[r, 1, last] = hy
            h[r, 2, last] = hz
            for k, d in enumerate(response(coef[0, last], dhy, dhz)):
                e[r, k, last] = e[r, k, last] + d
            note_top(e, rec, r, last, step, rows)
            a1y = above[0][1][r] + inv_far * hz
            a1z = above[1][1][r] - inv_far * hy
            magnetic_full(e, h, r, last - 1, (e[r, 1, last], e[r, 2, last]))
            magnetic_full(e, h, r, last, (a1y, a1z))
            polarize_step(e, p, j, coef, r, last)
            for x in (last - 1, last):
                electric_step(e, h, j, coef, r, x, (h[r, 1, x - 1], h[r, 2, x - 1]))
                note_top(e, rec, r, x, step + 1, rows)
        if not final:
            pack_edges((e, h, p, j), refs[5], rows, (last - 1, last))

    def lower():
        below = arrived(*wrap_phase(cs, 0, "gx", False))
        for r in range(2):
            dhy, dhz = courant * e0[r, 1], 0.0 - courant * e0[r, 0]
            e[r, 1, 0] = e[r, 1, 0] + coef[0, 0] * (below[1][0][r] + dhz)
            e[r, 2, 0] = e[r, 2, 0] - coef[0, 0] * (below[0][0][r] + dhy)
            dex, dey, dez = response(inv_far, dhy, dhz)
            hy, hz = magnetic_open(dex, dey, dez, dhy, dhz)
            b1y = below[0][1][r] + hy + courant * e[r, 2, 0]
            b1z = below[1][1][r] + hz - courant * e[r, 1, 0]
            magnetic_full(e, h, r, 0, (e[r, 1, 1], e[r, 2, 1]))
            polarize_step(e, p, j, coef, r, 0)
            electric_step(e, h, j, coef, r, 0, (b1y, b1z))
            electric_step(e, h, j, coef, r, 1, (h[r, 1, 0], h[r, 2, 0]))
            for x in range(2):
                note_top(e, rec, r, x, step + 1, rows)
        if not final:
            pack_edges((e, h, p, j), refs[5], rows, (0, 1))

    by_side(which, upper, lower)


def harmonics_body(rec, waves, harm):
    wave = waves[lax.axis_index("gy")]
    for x in range(rec.shape[1]):
        re, im = (
            jnp.dot(wave, rec[r, x], precision=lax.Precision.HIGHEST, preferred_element_type=jnp.float32)
            for r in range(2)
        )
        harm[0, x] = re[0:HARM] + im[HARM:]
        harm[1, x] = im[0:HARM] - re[HARM:]


def call(body, ins, outs, aliases=None, smem=(), hbm_in=(), hbm_out=False, scratch=(), cost=0):
    shapes = [jax.ShapeDtypeStruct(s, d) for s, d in outs]
    ins = [pltpu.with_memory_space_constraint(v, pltpu.HBM) if i in hbm_in else v for i, v in enumerate(ins)]
    vm = pl.BlockSpec(memory_space=pltpu.VMEM)
    sm = pl.BlockSpec(memory_space=pltpu.SMEM)
    hbm = pl.BlockSpec(memory_space=pltpu.HBM)
    return pl.pallas_call(
        body,
        out_shape=shapes,
        in_specs=[sm if i in smem else hbm if i in hbm_in else vm for i in range(len(ins))],
        out_specs=[hbm if hbm_out else vm] * len(outs),
        input_output_aliases=aliases or {},
        scratch_shapes=list(scratch),
        cost_estimate=pl.CostEstimate(flops=cost, bytes_accessed=cost, transcendentals=0),
        compiler_params=pltpu.CompilerParams(vmem_limit_bytes=VMEM_LIMIT),
    )(*ins)


def swap(block, axis, shift):
    count = lax.axis_size(axis)
    pairs = [(i % count, (i + 1) % count) for i in range(shift, count, 2)]
    return lax.ppermute(block, axis, [q for a, b in pairs for q in ((a, b), (b, a))])


def per_device(
    electric, magnetic, polarize, currents, material, pole_of, eps_inf, pole_decay, pole_freq, pole_strength, bloch
):
    parts, comps, planes, rows, depth = electric.shape
    count_x, count_y = lax.axis_size("gx"), lax.axis_size("gy")
    assert count_x % 2 == 0 and count_y == 2 and planes == 4
    width_y = rows * count_y
    f32 = jnp.float32
    ext = (rows + EDGE, depth)
    angle = 2.0 * math.pi / width_y * (np.arange(HARM)[:, None] * np.arange(width_y)[None, :] % width_y)
    waves = np.concatenate([np.cos(angle), np.sin(angle)]) / math.sqrt(width_y)
    waves = jnp.asarray(np.stack(np.split(waves, count_y, axis=1)).astype(np.float32))

    state_shape = ((parts, comps, planes) + ext, f32)
    coef_shape = ((4, planes) + ext, f32)
    tiles = 2 * 2 * comps * planes
    e, h, p, j, mat, edges = call(
        functools.partial(start_body, rows),
        (electric, magnetic, polarize, currents, material),
        [state_shape] * 4 + [(material.shape, material.dtype), ((tiles + planes, 8, depth), f32)],
        hbm_in=range(5),
        scratch=[pltpu.SemaphoreType.DMA((5,))],
    )
    tables = (pole_of, eps_inf, pole_decay, pole_freq, pole_strength)
    coef, cs, rec = call(
        functools.partial(coef_body, rows),
        (mat,) + tables + (bloch,),
        [coef_shape, ((4, 8, depth), f32), ((2, planes, rows, 128), f32)],
        smem=range(1, 7),
        cost=1 << 20,
    )
    far = [None, None]
    e0 = [None, None]
    msg = [None, None]
    state = (e, h, p, j)
    keep = [state_shape] * 4
    e0_shape = ((2, 2) + ext, f32)
    side_edges = swap(edges, "gy", 0)
    size = 8 * rows + 16
    rec_shape = (rec.shape, f32)
    for which in ORDER:
        if which == ORDER[0]:
            ins = (cs, side_edges) + tables + state + (coef,)
            *state, coef, e0[which], out = call(
                lambda *refs, which=which: send_body(rows, which, True, 0, refs),
                ins,
                keep + [coef_shape, e0_shape, ((size + rows + EDGE, depth), f32)],
                {7 + i: i for i in range(5)},
                smem=range(2, 7),
            )
        else:
            *state, e0[which], out, rec = call(
                lambda *refs, which=which: send_body(rows, which, True, 0, refs),
                tuple(state) + (coef, rec),
                keep + [e0_shape, ((size + rows + EDGE, depth), f32), rec_shape],
                {0: 0, 1: 1, 2: 2, 3: 3, 5: 6},
            )
        msg[which] = far[which] = swap(out, "gx", which)
    for step in range(0, STEPS, 2):
        final = step == STEPS - 2
        for which in ORDER:
            edge_shape = [] if final else [((tiles // 2, 8, depth), f32)]
            *state, rec = call(
                lambda *refs, which=which, step=step, final=final: finish_body(rows, which, step, final, refs),
                (cs, msg[which], e0[which], far[which], coef) + tuple(state) + (rec,),
                keep + [rec_shape] + edge_shape,
                {5 + i: i for i in range(5)},
            )
            if final:
                continue
            side_edges = swap(rec, "gy", 0)
            rec = state.pop()
            second = which == ORDER[1]
            *state, e0[which], out = call(
                lambda *refs, which=which, step=step: send_body(rows, which, False, step + 2, refs),
                (cs, side_edges) + tuple(state) + (coef,) + ((rec,) if second else ()),
                keep + [e0_shape, ((size, depth), f32)] + ([rec_shape] if second else []),
                {2: 0, 3: 1, 4: 2, 5: 3, **({7: 6} if second else {})},
            )
            if second:
                rec, out = out, e0[which]
                e0[which] = state.pop()
            msg[which] = swap(out, "gx", which)
    e, h, p, j = state
    (harm,) = call(harmonics_body, (rec, waves), [((2, planes, HARM, 128), f32)])
    other = swap(harm, "gy", 0)
    fields = call(
        functools.partial(store_body, rows),
        (e, h, p, j),
        [(electric.shape, f32)] * 4,
        hbm_out=True,
        scratch=[pltpu.SemaphoreType.DMA((4,))],
        cost=1 << 22,
    )
    (panel,) = call(panel_body, (harm, other), [((2, STEPS, planes, HARM), f32)])
    return (*fields, jnp.transpose(panel, (0, 1, 3, 2)))


def solution(mesh):
    field = P("angle", None, "gx", "gy", None)
    in_specs = (field,) * 4 + (P("gx", "gy", None),) + (P(),) * 5 + (P("angle"),)
    out_specs = (field,) * 4 + (P("angle", None, None, "gx"),)
    return jax.shard_map(per_device, mesh=mesh, in_specs=in_specs, out_specs=out_specs, check_vma=False)
```

```python
import functools
import math

import jax
import jax.numpy as jnp
import numpy as np
from jax import lax
from jax.experimental import pallas as pl
from jax.experimental.pallas import tpu as pltpu
from jax.sharding import PartitionSpec as P

STEPS = 8
HARM = 8
EDGE = 8
ORDER = (0, 1)
courant = 0.5
VMEM_LIMIT = 8 << 20


def next_y(v):
    return pltpu.roll(v, v.shape[0] - 1, 0)


def prev_y(v):
    return pltpu.roll(v, 1, 0)


def next_z(v):
    lane = lax.broadcasted_iota(jnp.int32, v.shape, 1)
    return jnp.where(lane == v.shape[1] - 1, 0.0, pltpu.roll(v, v.shape[1] - 1, 1))


def prev_z(v):
    lane = lax.broadcasted_iota(jnp.int32, v.shape, 1)
    return jnp.where(lane == 0, 0.0, pltpu.roll(v, 1, 1))


def turn(pair, cos_v, sin_v):
    return cos_v * pair[0] - sin_v * pair[1], sin_v * pair[0] + cos_v * pair[1]


def sublane(v):
    return lax.broadcasted_iota(jnp.int32, v.shape, 0)


def weave(first, second):
    row = sublane(first)
    return jnp.where((row < 2) | (row >= 6), first, pltpu.roll(second, 4, 0))


def edge_rows(ref, at, rows):
    low = ref[at + (slice(0, 8),)]
    high = ref[at + (slice(rows - 8, rows),)]
    return jnp.where(sublane(low) < 4, low, high)


def pack_edges(fields, out, rows, xs):
    e, h, p, j = fields
    for r in range(2):
        for g, (one, two) in enumerate(((e, h), (p, j))):
            for k in range(3):
                for i, x in enumerate(xs):
                    at = (r, k, x)
                    tile = weave(edge_rows(one, at, rows), edge_rows(two, at, rows))
                    out[((r * 2 + g) * 3 + k) * len(xs) + i] = tile


def wrap_phase(cs, axis, name, up):
    at, count = lax.axis_index(name), lax.axis_size(name)
    wraps = at == (count - 1 if up else 0)
    sine = cs[2 + axis, 0:1]
    return jnp.where(wraps, cs[axis, 0:1], 1.0), jnp.where(wraps, sine if up else 0.0 - sine, 0.0)


def unpack_edges(recv, fields, cs, rows, xs):
    e, h, p, j = fields
    up, dn = wrap_phase(cs, 1, "gy", True), wrap_phase(cs, 1, "gy", False)
    depth = e.shape[4]
    row = lax.broadcasted_iota(jnp.int32, (8, depth), 0)
    cos_v = jnp.where(row < 4, up[0], dn[0])
    sin_v = jnp.where(row < 4, up[1], dn[1])
    for g, (one, two) in enumerate(((e, h), (p, j))):
        for k in range(3):
            for i, x in enumerate(xs):
                pair = [recv[((r * 2 + g) * 3 + k) * len(xs) + i] for r in range(2)]
                for dst in (one, two):
                    re, im = turn(pair, cos_v, sin_v)
                    dst[0, k, x, rows:] = re
                    dst[1, k, x, rows:] = im
                    pair = [pltpu.roll(v, 4, 0) for v in pair]


def curl_e_x(ey, ez):
    return (next_y(ez) - ez) - (next_z(ey) - ey)


def magnetic_full(e, h, r, x, nxt):
    ex, ey, ez = (e[r, k, x] for k in range(3))
    ny_, nz_ = nxt
    h[r, 0, x] = h[r, 0, x] - courant * curl_e_x(ey, ez)
    h[r, 1, x] = h[r, 1, x] - courant * ((next_z(ex) - ex) - (nz_ - ez))
    h[r, 2, x] = h[r, 2, x] - courant * ((ny_ - ey) - (next_y(ex) - ex))


def magnetic_open(ex, ey, ez, hy, hz):
    hy = hy - courant * ((next_z(ex) - ex) + ez)
    hz = hz - courant * ((0.0 - ey) - (next_y(ex) - ex))
    return hy, hz


def polarize_step(e, p, j, coef, r, x):
    for k in range(3):
        now = coef[1, x] * j[r, k, x] + coef[2, x] * (coef[3, x] * e[r, k, x] - p[r, k, x])
        j[r, k, x] = now
        p[r, k, x] = p[r, k, x] + courant * now


def electric_step(e, h, j, coef, r, x, prev):
    hx, hy, hz = (h[r, k, x] for k in range(3))
    inv = coef[0, x]
    e[r, 0, x] = e[r, 0, x] + inv * ((hz - prev_y(hz)) - (hy - prev_z(hy)) - j[r, 0, x])
    dz, dy = hz, hy
    if prev is not None:
        dz, dy = hz - prev[1], hy - prev[0]
    e[r, 1, x] = e[r, 1, x] + inv * ((hx - prev_z(hx)) - dz - j[r, 1, x])
    e[r, 2, x] = e[r, 2, x] + inv * (dy - (hx - prev_y(hx)) - j[r, 2, x])


def response(inv, dhy, dhz):
    dex = inv * ((dhz - prev_y(dhz)) - (dhy - prev_z(dhy)))
    return dex, 0.0 - inv * dhz, inv * dhy


def note_top(e, rec, r, x, step, rows):
    depth = e.shape[4]
    top = e[r, 0, x, 0:rows, depth - 128 :]
    lane = lax.broadcasted_iota(jnp.int32, top.shape, 1)
    rec[r, x] = jnp.where(lane == step, pltpu.roll(top, (step + 1) % 128, 1), rec[r, x])


def start_body(rows, e_in, h_in, p_in, j_in, mat_in, e, h, p, j, mat, edges, sems):
    pairs = [(src, dst.at[:, :, :, 0:rows]) for src, dst in ((e_in, e), (h_in, h), (p_in, p), (j_in, j))]
    copies = [pltpu.make_async_copy(src, dst, sems.at[i]) for i, (src, dst) in enumerate(pairs + [(mat_in, mat)])]
    for c in copies:
        c.start()
    for dst in (e, h, p, j):
        dst[:, :, :, rows:] = jnp.zeros(dst.shape[:3] + (EDGE, dst.shape[4]), jnp.float32)
    for c in copies:
        c.wait()
    pack_edges((e, h, p, j), edges, rows, range(e.shape[2]))
    base = 2 * 2 * 3 * e.shape[2]
    for x in range(e.shape[2]):
        edges[base + x] = edge_rows(mat, (x,), rows).astype(jnp.float32)


def store_body(rows, e, h, p, j, e_out, h_out, p_out, j_out, sems):
    pairs = ((e, e_out), (h, h_out), (p, p_out), (j, j_out))
    copies = [
        pltpu.make_async_copy(src.at[:, :, :, 0:rows], dst, sems.at[i]) for i, (src, dst) in enumerate(pairs)
    ]
    for c in copies:
        c.start()
    for c in copies:
        c.wait()


def panel_body(own, other, out):
    for r in range(2):
        for x in range(own.shape[1]):
            out[r, :, x] = jnp.transpose(own[r, x] + other[r, x])[0:STEPS]


def cell_tables(kind, pole_of, eps, dec, frq, stg):
    vals = [jnp.full(kind.shape, t, jnp.float32) for t in (eps[0], dec[pole_of[0]], frq[pole_of[0]], stg[pole_of[0]])]
    for m in range(1, eps.shape[0]):
        hit = kind == m
        pole = pole_of[m]
        for i, t in enumerate((eps[m], dec[pole], frq[pole], stg[pole])):
            vals[i] = jnp.where(hit, t, vals[i])
    vals[0] = courant / vals[0]
    return vals


def coef_body(rows, mat, pole_of, eps, dec, frq, stg, bloch, coef, cs, rec):
    rec[...] = jnp.zeros(rec.shape, jnp.float32)
    for i in range(2):
        turns = jnp.full(cs.shape[1:], bloch[i], jnp.float32)
        cs[i] = jnp.cos(turns)
        cs[2 + i] = jnp.sin(turns)
    for x in range(mat.shape[0]):
        for y in range(0, rows, 8):
            vals = cell_tables(mat[x, y : y + 8], pole_of, eps, dec, frq, stg)
            for i in range(4):
                coef[i, x, y : y + 8] = vals[i]
        for i in range(4):
            coef[i, x, rows:] = jnp.zeros((EDGE, coef.shape[3]), jnp.float32)


def by_side(which, upper, lower):
    mine = lax.axis_index("gx") % 2 == which
    pl.when(mine)(upper)
    pl.when(jnp.logical_not(mine))(lower)


def send_body(rows, which, first, step, refs):
    refs = list(refs)
    second = which == ORDER[1]
    if second:
        rec = refs.pop()
        refs.pop(5 if first else 7)
    if first and which == ORDER[0]:
        cs, edges, pole_of, eps, dec, frq, stg = refs[0:7]
        e, h, p, j, coef, e0, out = refs[12:]
    elif first:
        e, h, p, j, e0, out = refs[5:]
        coef = refs[4]
    else:
        cs, edges = refs[0:2]
        coef = refs[6]
        e, h, p, j, e0, out = refs[7:]
    planes = e.shape[2]
    last = planes - 1
    half = 4 * rows
    if first and which == ORDER[0]:
        unpack_edges(edges, (e, h, p, j), cs, rows, range(planes))
        base = 2 * 2 * 3 * planes
        for x in range(planes):
            kind = edges[base + x].astype(jnp.int32)
            vals = cell_tables(kind, pole_of, eps, dec, frq, stg)
            for i in range(4):
                coef[i, x, rows:] = vals[i]

    def upper():
        if not first:
            unpack_edges(edges, (e, h, p, j), cs, rows, (last - 1, last))
        for r in range(2):
            tiles = []
            magnetic_full(e, h, r, last - 1, (e[r, 1, last], e[r, 2, last]))
            ex, ey, ez = (e[r, k, last] for k in range(3))
            h[r, 0, last] = h[r, 0, last] - courant * curl_e_x(ey, ez)
            hs = magnetic_open(ex, ey, ez, h[r, 1, last], h[r, 2, last])
            for k in range(2):
                h[r, 1 + k, last] = hs[k]
                out[(2 * r + k) * rows : (2 * r + k + 1) * rows] = hs[k][0:rows]
                tiles.append(hs[k][rows:])
            polarize_step(e, p, j, coef, r, last)
            electric_step(e, h, j, coef, r, last, (h[r, 1, last - 1], h[r, 2, last - 1]))
            ex, ey, ez = (e[r, k, last] for k in range(3))
            hs = magnetic_open(ex, ey, ez, h[r, 1, last], h[r, 2, last])
            for k in range(2):
                at = half + (2 * r + k) * rows
                out[at : at + rows] = hs[k][0:rows]
            at = 2 * half + 8 * r
            out[at : at + 8] = weave(*tiles)
        if first:
            out[2 * half + 16 :] = coef[0, last]

    def lower():
        if not first:
            unpack_edges(edges, (e, h, p, j), cs, rows, (0, 1))
        for r in range(2):
            tiles = []
            magnetic_full(e, h, r, 0, (e[r, 1, 1], e[r, 2, 1]))
            for k in range(2):
                now = e[r, 1 + k, 0]
                e0[r, k] = now
                out[(2 * r + k) * rows : (2 * r + k + 1) * rows] = now[0:rows]
                tiles.append(now[rows:])
            polarize_step(e, p, j, coef, r, 0)
            electric_step(e, h, j, coef, r, 0, None)
            for k in range(2):
                at = half + (2 * r + k) * rows
                now = e[r, 1 + k, 0]
                out[at : at + rows] = now[0:rows]
                row = sublane(tiles[k])
                tiles[k] = jnp.where(row == 1, pltpu.roll(now[rows:], 2, 0), tiles[k])
            at = 2 * half + 8 * r
            out[at : at + 8] = weave(*tiles)
        if first:
            out[2 * half + 16 :] = coef[0, 0]

    by_side(which, upper, lower)
    if second:
        inner_part(rows, step, (e, h, p, j, rec), coef)


def inner_part(rows, step, state, coef):
    e, h, p, j, rec = state
    planes = e.shape[2]
    for r in range(2):
        for x in range(1, planes - 2):
            magnetic_full(e, h, r, x, (e[r, 1, x + 1], e[r, 2, x + 1]))
        for x in range(1, planes - 1):
            polarize_step(e, p, j, coef, r, x)
            electric_step(e, h, j, coef, r, x, (h[r, 1, x - 1], h[r, 2, x - 1]))
        for x in range(planes - 1):
            note_top(e, rec, r, x, step, rows)
        for x in range(1, planes - 2):
            magnetic_full(e, h, r, x, (e[r, 1, x + 1], e[r, 2, x + 1]))
        for x in range(1, planes - 1):
            polarize_step(e, p, j, coef, r, x)


def finish_body(rows, which, step, final, refs):
    cs, msg, e0, far, coef = refs[0:5]
    refs = refs[10:]
    e, h, p, j, rec = refs[0:5]
    planes = e.shape[2]
    last = planes - 1
    half = 4 * rows
    inv_far = far[2 * half + 16 : 2 * half + 16 + rows + EDGE]

    def arrived(cos_v, sin_v):
        res = []
        for k in range(2):
            raw = []
            for r in range(2):
                tile = msg[2 * half + 8 * r : 2 * half + 8 * r + 8]
                if k == 1:
                    tile = pltpu.roll(tile, 4, 0)
                at = (2 * r + k) * rows
                one = jnp.concatenate([msg[at : at + rows], tile], axis=0)
                two = jnp.concatenate([msg[half + at : half + at + rows], pltpu.roll(tile, 6, 0)], axis=0)
                raw.append((one, two))
            res.append((turn((raw[0][0], raw[1][0]), cos_v, sin_v), turn((raw[0][1], raw[1][1]), cos_v, sin_v)))
        return res

    def upper():
        above = arrived(*wrap_phase(cs, 0, "gx", True))
        for r in range(2):
            a0y, a0z = above[0][0][r], above[1][0][r]
            dhy, dhz = courant * a0z, 0.0 - courant * a0y
            hy = h[r, 1, last] + dhy
            hz = h[r, 2, last] + dhz
            h[r, 1, last] = hy
            h[r, 2, last] = hz
            for k, d in enumerate(response(coef[0, last], dhy, dhz)):
                e[r, k, last] = e[r, k, last] + d
            note_top(e, rec, r, last, step, rows)
            a1y = above[0][1][r] + inv_far * hz
            a1z = above[1][1][r] - inv_far * hy
            magnetic_full(e, h, r, last - 1, (e[r, 1, last], e[r, 2, last]))
            magnetic_full(e, h, r, last, (a1y, a1z))
            polarize_step(e, p, j, coef, r, last)
            for x in (last - 1, last):
                electric_step(e, h, j, coef, r, x, (h[r, 1, x - 1], h[r, 2, x - 1]))
                note_top(e, rec, r, x, step + 1, rows)
        if not final:
            pack_edges((e, h, p, j), refs[5], rows, (last - 1, last))

    def lower():
        below = arrived(*wrap_phase(cs, 0, "gx", False))
        for r in range(2):
            dhy, dhz = courant * e0[r, 1], 0.0 - courant * e0[r, 0]
            e[r, 1, 0] = e[r, 1, 0] + coef[0, 0] * (below[1][0][r] + dhz)
            e[r, 2, 0] = e[r, 2, 0] - coef[0, 0] * (below[0][0][r] + dhy)
            dex, dey, dez = response(inv_far, dhy, dhz)
            hy, hz = magnetic_open(dex, dey, dez, dhy, dhz)
            b1y = below[0][1][r] + hy + courant * e[r, 2, 0]
            b1z = below[1][1][r] + hz - courant * e[r, 1, 0]
            magnetic_full(e, h, r, 0, (e[r, 1, 1], e[r, 2, 1]))
            polarize_step(e, p, j, coef, r, 0)
            electric_step(e, h, j, coef, r, 0, (b1y, b1z))
            electric_step(e, h, j, coef, r, 1, (h[r, 1, 0], h[r, 2, 0]))
            for x in range(2):
                note_top(e, rec, r, x, step + 1, rows)
        if not final:
            pack_edges((e, h, p, j), refs[5], rows, (0, 1))

    by_side(which, upper, lower)


def harmonics_body(rec, waves, harm):
    wave = waves[lax.axis_index("gy")]
    for x in range(rec.shape[1]):
        re, im = (
            jnp.dot(wave, rec[r, x], precision=lax.Precision.HIGHEST, preferred_element_type=jnp.float32)
            for r in range(2)
        )
        harm[0, x] = re[0:HARM] + im[HARM:]
        harm[1, x] = im[0:HARM] - re[HARM:]


def call(body, ins, outs, aliases=None, smem=(), hbm_in=(), hbm_out=False, scratch=(), cost=0):
    shapes = [jax.ShapeDtypeStruct(s, d) for s, d in outs]
    ins = [pltpu.with_memory_space_constraint(v, pltpu.HBM) if i in hbm_in else v for i, v in enumerate(ins)]
    vm = pl.BlockSpec(memory_space=pltpu.VMEM)
    sm = pl.BlockSpec(memory_space=pltpu.SMEM)
    hbm = pl.BlockSpec(memory_space=pltpu.HBM)
    return pl.pallas_call(
        body,
        out_shape=shapes,
        in_specs=[sm if i in smem else hbm if i in hbm_in else vm for i in range(len(ins))],
        out_specs=[hbm if hbm_out else vm] * len(outs),
        input_output_aliases=aliases or {},
        scratch_shapes=list(scratch),
        cost_estimate=pl.CostEstimate(flops=cost, bytes_accessed=cost, transcendentals=0),
        compiler_params=pltpu.CompilerParams(vmem_limit_bytes=VMEM_LIMIT),
    )(*ins)


def swap(block, axis, shift):
    count = lax.axis_size(axis)
    pairs = [(i % count, (i + 1) % count) for i in range(shift, count, 2)]
    return lax.ppermute(block, axis, [q for a, b in pairs for q in ((a, b), (b, a))])


def per_device(
    electric, magnetic, polarize, currents, material, pole_of, eps_inf, pole_decay, pole_freq, pole_strength, bloch
):
    parts, comps, planes, rows, depth = electric.shape
    count_x, count_y = lax.axis_size("gx"), lax.axis_size("gy")
    assert count_x % 2 == 0 and count_y == 2 and planes == 4
    width_y = rows * count_y
    f32 = jnp.float32
    ext = (rows + EDGE, depth)
    angle = 2.0 * math.pi / width_y * (np.arange(HARM)[:, None] * np.arange(width_y)[None, :] % width_y)
    waves = np.concatenate([np.cos(angle), np.sin(angle)]) / math.sqrt(width_y)
    waves = jnp.asarray(np.stack(np.split(waves, count_y, axis=1)).astype(np.float32))

    state_shape = ((parts, comps, planes) + ext, f32)
    coef_shape = ((4, planes) + ext, f32)
    tiles = 2 * 2 * comps * planes
    e, h, p, j, mat, edges = call(
        functools.partial(start_body, rows),
        (electric, magnetic, polarize, currents, material),
        [state_shape] * 4 + [(material.shape, material.dtype), ((tiles + planes, 8, depth), f32)],
        hbm_in=range(5),
        scratch=[pltpu.SemaphoreType.DMA((5,))],
    )
    tables = (pole_of, eps_inf, pole_decay, pole_freq, pole_strength)
    coef, cs, rec = call(
        functools.partial(coef_body, rows),
        (mat,) + tables + (bloch,),
        [coef_shape, ((4, 8, depth), f32), ((2, planes, rows, 128), f32)],
        smem=range(1, 7),
        cost=1 << 20,
    )
    far = [None, None]
    e0 = [None, None]
    msg = [None, None]
    state = (e, h, p, j)
    keep = [state_shape] * 4
    e0_shape = ((2, 2) + ext, f32)
    side_edges = swap(edges, "gy", 0)
    size = 8 * rows + 16
    rec_shape = (rec.shape, f32)
    for which in ORDER:
        if which == ORDER[0]:
            ins = (cs, side_edges) + tables + state + (coef,)
            *state, coef, e0[which], out = call(
                lambda *refs, which=which: send_body(rows, which, True, 0, refs),
                ins,
                keep + [coef_shape, e0_shape, ((size + rows + EDGE, depth), f32)],
                {7 + i: i for i in range(5)},
                smem=range(2, 7),
            )
        else:
            *state, e0[which], out, rec = call(
                lambda *refs, which=which: send_body(rows, which, True, 0, refs),
                tuple(state) + (coef, rec),
                keep + [e0_shape, ((size + rows + EDGE, depth), f32), rec_shape],
                {0: 0, 1: 1, 2: 2, 3: 3, 5: 6},
            )
            out, msg[ORDER[0]] = lax.optimization_barrier((out, msg[ORDER[0]]))
        msg[which] = far[which] = swap(out, "gx", which)
    for step in range(0, STEPS, 2):
        final = step == STEPS - 2
        for which in ORDER:
            edge_shape = [] if final else [((tiles // 2, 8, depth), f32)]
            *state, rec = call(
                lambda *refs, which=which, step=step, final=final: finish_body(rows, which, step, final, refs),
                (cs, msg[which], e0[which], far[which], coef) + tuple(state) + (rec,),
                keep + [rec_shape] + edge_shape,
                {5 + i: i for i in range(5)},
            )
            if final:
                continue
            side_edges = swap(rec, "gy", 0)
            rec = state.pop()
            second = which == ORDER[1]
            *state, e0[which], out = call(
                lambda *refs, which=which, step=step: send_body(rows, which, False, step + 2, refs),
                (cs, side_edges) + tuple(state) + (coef,) + ((rec,) if second else ()),
                keep + [e0_shape, ((size, depth), f32)] + ([rec_shape] if second else []),
                {2: 0, 3: 1, 4: 2, 5: 3, **({7: 6} if second else {})},
            )
            if second:
                rec, out = out, e0[which]
                e0[which] = state.pop()
            msg[which] = swap(out, "gx", which)
    e, h, p, j = state
    (harm,) = call(harmonics_body, (rec, waves), [((2, planes, HARM, 128), f32)])
    other = swap(harm, "gy", 0)
    fields = call(
        functools.partial(store_body, rows),
        (e, h, p, j),
        [(electric.shape, f32)] * 4,
        hbm_out=True,
        scratch=[pltpu.SemaphoreType.DMA((4,))],
        cost=1 << 22,
    )
    (panel,) = call(panel_body, (harm, other), [((2, STEPS, planes, HARM), f32)])
    return (*fields, jnp.transpose(panel, (0, 1, 3, 2)))


def solution(mesh):
    field = P("angle", None, "gx", "gy", None)
    in_specs = (field,) * 4 + (P("gx", "gy", None),) + (P(),) * 5 + (P("angle"),)
    out_specs = (field,) * 4 + (P("angle", None, None, "gx"),)
    return jax.shard_map(per_device, mesh=mesh, in_specs=in_specs, out_specs=out_specs, check_vma=False)
```

```python
import functools
import math

import jax
import jax.numpy as jnp
import numpy as np
from jax import lax
from jax.experimental import pallas as pl
from jax.experimental.pallas import tpu as pltpu
from jax.sharding import PartitionSpec as P

STEPS = 8
HARM = 8
EDGE = 8
ORDER = (0, 1)
courant = 0.5
VMEM_LIMIT = 8 << 20


def next_y(v):
    return pltpu.roll(v, v.shape[0] - 1, 0)


def prev_y(v):
    return pltpu.roll(v, 1, 0)


def next_z(v):
    lane = lax.broadcasted_iota(jnp.int32, v.shape, 1)
    return jnp.where(lane == v.shape[1] - 1, 0.0, pltpu.roll(v, v.shape[1] - 1, 1))


def prev_z(v):
    lane = lax.broadcasted_iota(jnp.int32, v.shape, 1)
    return jnp.where(lane == 0, 0.0, pltpu.roll(v, 1, 1))


def turn(pair, cos_v, sin_v):
    return cos_v * pair[0] - sin_v * pair[1], sin_v * pair[0] + cos_v * pair[1]


def sublane(v):
    return lax.broadcasted_iota(jnp.int32, v.shape, 0)


def weave(first, second):
    row = sublane(first)
    return jnp.where((row < 2) | (row >= 6), first, pltpu.roll(second, 4, 0))


def edge_rows(ref, at, rows):
    low = ref[at + (slice(0, 8),)]
    high = ref[at + (slice(rows - 8, rows),)]
    return jnp.where(sublane(low) < 4, low, high)


def pack_edges(fields, out, rows, xs):
    e, h, p, j = fields
    for r in range(2):
        for g, (one, two) in enumerate(((e, h), (p, j))):
            for k in range(3):
                for i, x in enumerate(xs):
                    at = (r, k, x)
                    tile = weave(edge_rows(one, at, rows), edge_rows(two, at, rows))
                    out[((r * 2 + g) * 3 + k) * len(xs) + i] = tile


def wrap_phase(cs, axis, name, up):
    at, count = lax.axis_index(name), lax.axis_size(name)
    wraps = at == (count - 1 if up else 0)
    sine = cs[2 + axis, 0:1]
    return jnp.where(wraps, cs[axis, 0:1], 1.0), jnp.where(wraps, sine if up else 0.0 - sine, 0.0)


def unpack_edges(recv, fields, cs, rows, xs):
    e, h, p, j = fields
    up, dn = wrap_phase(cs, 1, "gy", True), wrap_phase(cs, 1, "gy", False)
    depth = e.shape[4]
    row = lax.broadcasted_iota(jnp.int32, (8, depth), 0)
    cos_v = jnp.where(row < 4, up[0], dn[0])
    sin_v = jnp.where(row < 4, up[1], dn[1])
    for g, (one, two) in enumerate(((e, h), (p, j))):
        for k in range(3):
            for i, x in enumerate(xs):
                pair = [recv[((r * 2 + g) * 3 + k) * len(xs) + i] for r in range(2)]
                for dst in (one, two):
                    re, im = turn(pair, cos_v, sin_v)
                    dst[0, k, x, rows:] = re
                    dst[1, k, x, rows:] = im
                    pair = [pltpu.roll(v, 4, 0) for v in pair]


def curl_e_x(ey, ez):
    return (next_y(ez) - ez) - (next_z(ey) - ey)


def magnetic_full(e, h, r, x, nxt):
    ex, ey, ez = (e[r, k, x] for k in range(3))
    ny_, nz_ = nxt
    h[r, 0, x] = h[r, 0, x] - courant * curl_e_x(ey, ez)
    h[r, 1, x] = h[r, 1, x] - courant * ((next_z(ex) - ex) - (nz_ - ez))
    h[r, 2, x] = h[r, 2, x] - courant * ((ny_ - ey) - (next_y(ex) - ex))


def magnetic_open(ex, ey, ez, hy, hz):
    hy = hy - courant * ((next_z(ex) - ex) + ez)
    hz = hz - courant * ((0.0 - ey) - (next_y(ex) - ex))
    return hy, hz


def polarize_step(e, p, j, coef, r, x):
    for k in range(3):
        now = coef[1, x] * j[r, k, x] + coef[2, x] * (coef[3, x] * e[r, k, x] - p[r, k, x])
        j[r, k, x] = now
        p[r, k, x] = p[r, k, x] + courant * now


def electric_step(e, h, j, coef, r, x, prev):
    hx, hy, hz = (h[r, k, x] for k in range(3))
    inv = coef[0, x]
    e[r, 0, x] = e[r, 0, x] + inv * ((hz - prev_y(hz)) - (hy - prev_z(hy)) - j[r, 0, x])
    dz, dy = hz, hy
    if prev is not None:
        dz, dy = hz - prev[1], hy - prev[0]
    e[r, 1, x] = e[r, 1, x] + inv * ((hx - prev_z(hx)) - dz - j[r, 1, x])
    e[r, 2, x] = e[r, 2, x] + inv * (dy - (hx - prev_y(hx)) - j[r, 2, x])


def response(inv, dhy, dhz):
    dex = inv * ((dhz - prev_y(dhz)) - (dhy - prev_z(dhy)))
    return dex, 0.0 - inv * dhz, inv * dhy


def note_top(e, rec, r, x, step, rows):
    depth = e.shape[4]
    top = e[r, 0, x, 0:rows, depth - 128 :]
    lane = lax.broadcasted_iota(jnp.int32, top.shape, 1)
    rec[r, x] = jnp.where(lane == step, pltpu.roll(top, (step + 1) % 128, 1), rec[r, x])


def start_body(rows, e_in, h_in, p_in, j_in, mat_in, e, h, p, j, mat, edges, sems):
    pairs = [(src, dst.at[:, :, :, 0:rows]) for src, dst in ((e_in, e), (h_in, h), (p_in, p), (j_in, j))]
    copies = [pltpu.make_async_copy(src, dst, sems.at[i]) for i, (src, dst) in enumerate(pairs + [(mat_in, mat)])]
    for c in copies:
        c.start()
    for dst in (e, h, p, j):
        dst[:, :, :, rows:] = jnp.zeros(dst.shape[:3] + (EDGE, dst.shape[4]), jnp.float32)
    for c in copies:
        c.wait()
    pack_edges((e, h, p, j), edges, rows, range(e.shape[2]))
    base = 2 * 2 * 3 * e.shape[2]
    for x in range(e.shape[2]):
        edges[base + x] = edge_rows(mat, (x,), rows).astype(jnp.float32)


def store_body(rows, e, h, p, j, e_out, h_out, p_out, j_out, sems):
    pairs = ((e, e_out), (h, h_out), (p, p_out), (j, j_out))
    copies = [
        pltpu.make_async_copy(src.at[:, :, :, 0:rows], dst, sems.at[i]) for i, (src, dst) in enumerate(pairs)
    ]
    for c in copies:
        c.start()
    for c in copies:
        c.wait()


def panel_body(own, other, out):
    for r in range(2):
        for x in range(own.shape[1]):
            out[r, :, x] = jnp.transpose(own[r, x] + other[r, x])[0:STEPS]


def cell_tables(kind, pole_of, eps, dec, frq, stg):
    vals = [jnp.full(kind.shape, t, jnp.float32) for t in (eps[0], dec[pole_of[0]], frq[pole_of[0]], stg[pole_of[0]])]
    for m in range(1, eps.shape[0]):
        hit = kind == m
        pole = pole_of[m]
        for i, t in enumerate((eps[m], dec[pole], frq[pole], stg[pole])):
            vals[i] = jnp.where(hit, t, vals[i])
    vals[0] = courant / vals[0]
    return vals


def coef_body(rows, mat, pole_of, eps, dec, frq, stg, bloch, coef, cs, rec):
    rec[...] = jnp.zeros(rec.shape, jnp.float32)
    for i in range(2):
        turns = jnp.full(cs.shape[1:], bloch[i], jnp.float32)
        cs[i] = jnp.cos(turns)
        cs[2 + i] = jnp.sin(turns)
    for x in range(mat.shape[0]):
        for y in range(0, rows, 8):
            vals = cell_tables(mat[x, y : y + 8], pole_of, eps, dec, frq, stg)
            for i in range(4):
                coef[i, x, y : y + 8] = vals[i]
        for i in range(4):
            coef[i, x, rows:] = jnp.zeros((EDGE, coef.shape[3]), jnp.float32)


def by_side(which, upper, lower):
    mine = lax.axis_index("gx") % 2 == which
    pl.when(mine)(upper)
    pl.when(jnp.logical_not(mine))(lower)


def send_body(rows, which, first, step, refs):
    refs = list(refs)
    second = which == ORDER[1]
    if second:
        rec = refs.pop()
        refs.pop(5 if first else 7)
    if first and which == ORDER[0]:
        cs, edges, pole_of, eps, dec, frq, stg = refs[0:7]
        e, h, p, j, coef, e0, out = refs[12:]
    elif first:
        e, h, p, j, e0, out = refs[5:]
        coef = refs[4]
    else:
        cs, edges = refs[0:2]
        coef = refs[6]
        e, h, p, j, e0, out = refs[7:]
    planes = e.shape[2]
    last = planes - 1
    half = 4 * rows
    if first and which == ORDER[0]:
        unpack_edges(edges, (e, h, p, j), cs, rows, range(planes))
        base = 2 * 2 * 3 * planes
        for x in range(planes):
            kind = edges[base + x].astype(jnp.int32)
            vals = cell_tables(kind, pole_of, eps, dec, frq, stg)
            for i in range(4):
                coef[i, x, rows:] = vals[i]

    def upper():
        if not first:
            unpack_edges(edges, (e, h, p, j), cs, rows, (last - 1, last))
        for r in range(2):
            tiles = []
            magnetic_full(e, h, r, last - 1, (e[r, 1, last], e[r, 2, last]))
            ex, ey, ez = (e[r, k, last] for k in range(3))
            h[r, 0, last] = h[r, 0, last] - courant * curl_e_x(ey, ez)
            hs = magnetic_open(ex, ey, ez, h[r, 1, last], h[r, 2, last])
            for k in range(2):
                h[r, 1 + k, last] = hs[k]
                out[(2 * r + k) * rows : (2 * r + k + 1) * rows] = hs[k][0:rows]
                tiles.append(hs[k][rows:])
            polarize_step(e, p, j, coef, r, last)
            electric_step(e, h, j, coef, r, last, (h[r, 1, last - 1], h[r, 2, last - 1]))
            ex, ey, ez = (e[r, k, last] for k in range(3))
            hs = magnetic_open(ex, ey, ez, h[r, 1, last], h[r, 2, last])
            for k in range(2):
                at = half + (2 * r + k) * rows
                out[at : at + rows] = hs[k][0:rows]
            at = 2 * half + 8 * r
            out[at : at + 8] = weave(*tiles)
        if first:
            out[2 * half + 16 :] = coef[0, last]

    def lower():
        if not first:
            unpack_edges(edges, (e, h, p, j), cs, rows, (0, 1))
        for r in range(2):
            tiles = []
            magnetic_full(e, h, r, 0, (e[r, 1, 1], e[r, 2, 1]))
            for k in range(2):
                now = e[r, 1 + k, 0]
                e0[r, k] = now
                out[(2 * r + k) * rows : (2 * r + k + 1) * rows] = now[0:rows]
                tiles.append(now[rows:])
            polarize_step(e, p, j, coef, r, 0)
            electric_step(e, h, j, coef, r, 0, None)
            for k in range(2):
                at = half + (2 * r + k) * rows
                now = e[r, 1 + k, 0]
                out[at : at + rows] = now[0:rows]
                row = sublane(tiles[k])
                tiles[k] = jnp.where(row == 1, pltpu.roll(now[rows:], 2, 0), tiles[k])
            at = 2 * half + 8 * r
            out[at : at + 8] = weave(*tiles)
        if first:
            out[2 * half + 16 :] = coef[0, 0]

    by_side(which, upper, lower)
    if second and step < STEPS - 2:
        inner_part(rows, step, (e, h, p, j, rec), coef)


def inner_part(rows, step, state, coef):
    e, h, p, j, rec = state
    planes = e.shape[2]
    for r in range(2):
        for x in range(1, planes - 2):
            magnetic_full(e, h, r, x, (e[r, 1, x + 1], e[r, 2, x + 1]))
        for x in range(1, planes - 1):
            polarize_step(e, p, j, coef, r, x)
            electric_step(e, h, j, coef, r, x, (h[r, 1, x - 1], h[r, 2, x - 1]))
        for x in range(planes - 1):
            note_top(e, rec, r, x, step, rows)
        for x in range(1, planes - 2):
            magnetic_full(e, h, r, x, (e[r, 1, x + 1], e[r, 2, x + 1]))
        for x in range(1, planes - 1):
            polarize_step(e, p, j, coef, r, x)


def finish_body(rows, which, step, final, refs):
    cs, msg, e0, far, coef = refs[0:5]
    refs = refs[10:]
    e, h, p, j, rec = refs[0:5]
    planes = e.shape[2]
    last = planes - 1
    half = 4 * rows
    inv_far = far[2 * half + 16 : 2 * half + 16 + rows + EDGE]

    def arrived(cos_v, sin_v):
        res = []
        for k in range(2):
            raw = []
            for r in range(2):
                tile = msg[2 * half + 8 * r : 2 * half + 8 * r + 8]
                if k == 1:
                    tile = pltpu.roll(tile, 4, 0)
                at = (2 * r + k) * rows
                one = jnp.concatenate([msg[at : at + rows], tile], axis=0)
                two = jnp.concatenate([msg[half + at : half + at + rows], pltpu.roll(tile, 6, 0)], axis=0)
                raw.append((one, two))
            res.append((turn((raw[0][0], raw[1][0]), cos_v, sin_v), turn((raw[0][1], raw[1][1]), cos_v, sin_v)))
        return res

    def upper():
        above = arrived(*wrap_phase(cs, 0, "gx", True))
        for r in range(2):
            a0y, a0z = above[0][0][r], above[1][0][r]
            dhy, dhz = courant * a0z, 0.0 - courant * a0y
            hy = h[r, 1, last] + dhy
            hz = h[r, 2, last] + dhz
            h[r, 1, last] = hy
            h[r, 2, last] = hz
            for k, d in enumerate(response(coef[0, last], dhy, dhz)):
                e[r, k, last] = e[r, k, last] + d
            note_top(e, rec, r, last, step, rows)
            a1y = above[0][1][r] + inv_far * hz
            a1z = above[1][1][r] - inv_far * hy
            magnetic_full(e, h, r, last - 1, (e[r, 1, last], e[r, 2, last]))
            magnetic_full(e, h, r, last, (a1y, a1z))
            polarize_step(e, p, j, coef, r, last)
            for x in (last - 1, last):
                electric_step(e, h, j, coef, r, x, (h[r, 1, x - 1], h[r, 2, x - 1]))
                note_top(e, rec, r, x, step + 1, rows)
        if not final:
            pack_edges((e, h, p, j), refs[5], rows, (last - 1, last))

    def lower():
        below = arrived(*wrap_phase(cs, 0, "gx", False))
        for r in range(2):
            dhy, dhz = courant * e0[r, 1], 0.0 - courant * e0[r, 0]
            e[r, 1, 0] = e[r, 1, 0] + coef[0, 0] * (below[1][0][r] + dhz)
            e[r, 2, 0] = e[r, 2, 0] - coef[0, 0] * (below[0][0][r] + dhy)
            dex, dey, dez = response(inv_far, dhy, dhz)
            hy, hz = magnetic_open(dex, dey, dez, dhy, dhz)
            b1y = below[0][1][r] + hy + courant * e[r, 2, 0]
            b1z = below[1][1][r] + hz - courant * e[r, 1, 0]
            magnetic_full(e, h, r, 0, (e[r, 1, 1], e[r, 2, 1]))
            polarize_step(e, p, j, coef, r, 0)
            electric_step(e, h, j, coef, r, 0, (b1y, b1z))
            electric_step(e, h, j, coef, r, 1, (h[r, 1, 0], h[r, 2, 0]))
            for x in range(2):
                note_top(e, rec, r, x, step + 1, rows)
        if not final:
            pack_edges((e, h, p, j), refs[5], rows, (0, 1))

    by_side(which, upper, lower)


def harmonics_body(rec, waves, harm):
    wave = waves[lax.axis_index("gy")]
    for x in range(rec.shape[1]):
        re, im = (
            jnp.dot(wave, rec[r, x], precision=lax.Precision.HIGHEST, preferred_element_type=jnp.float32)
            for r in range(2)
        )
        harm[0, x] = re[0:HARM] + im[HARM:]
        harm[1, x] = im[0:HARM] - re[HARM:]


def call(body, ins, outs, aliases=None, smem=(), hbm_in=(), hbm_out=False, scratch=(), cost=0):
    shapes = [jax.ShapeDtypeStruct(s, d) for s, d in outs]
    ins = [pltpu.with_memory_space_constraint(v, pltpu.HBM) if i in hbm_in else v for i, v in enumerate(ins)]
    vm = pl.BlockSpec(memory_space=pltpu.VMEM)
    sm = pl.BlockSpec(memory_space=pltpu.SMEM)
    hbm = pl.BlockSpec(memory_space=pltpu.HBM)
    return pl.pallas_call(
        body,
        out_shape=shapes,
        in_specs=[sm if i in smem else hbm if i in hbm_in else vm for i in range(len(ins))],
        out_specs=[hbm if hbm_out else vm] * len(outs),
        input_output_aliases=aliases or {},
        scratch_shapes=list(scratch),
        cost_estimate=pl.CostEstimate(flops=cost, bytes_accessed=cost, transcendentals=0),
        compiler_params=pltpu.CompilerParams(vmem_limit_bytes=VMEM_LIMIT),
    )(*ins)


def swap(block, axis, shift):
    count = lax.axis_size(axis)
    pairs = [(i % count, (i + 1) % count) for i in range(shift, count, 2)]
    return lax.ppermute(block, axis, [q for a, b in pairs for q in ((a, b), (b, a))])


def per_device(
    electric, magnetic, polarize, currents, material, pole_of, eps_inf, pole_decay, pole_freq, pole_strength, bloch
):
    parts, comps, planes, rows, depth = electric.shape
    count_x, count_y = lax.axis_size("gx"), lax.axis_size("gy")
    assert count_x % 2 == 0 and count_y == 2 and planes == 4
    width_y = rows * count_y
    f32 = jnp.float32
    ext = (rows + EDGE, depth)
    angle = 2.0 * math.pi / width_y * (np.arange(HARM)[:, None] * np.arange(width_y)[None, :] % width_y)
    waves = np.concatenate([np.cos(angle), np.sin(angle)]) / math.sqrt(width_y)
    waves = jnp.asarray(np.stack(np.split(waves, count_y, axis=1)).astype(np.float32))

    state_shape = ((parts, comps, planes) + ext, f32)
    coef_shape = ((4, planes) + ext, f32)
    tiles = 2 * 2 * comps * planes
    e, h, p, j, mat, edges = call(
        functools.partial(start_body, rows),
        (electric, magnetic, polarize, currents, material),
        [state_shape] * 4 + [(material.shape, material.dtype), ((tiles + planes, 8, depth), f32)],
        hbm_in=range(5),
        scratch=[pltpu.SemaphoreType.DMA((5,))],
    )
    tables = (pole_of, eps_inf, pole_decay, pole_freq, pole_strength)
    coef, cs, rec = call(
        functools.partial(coef_body, rows),
        (mat,) + tables + (bloch,),
        [coef_shape, ((4, 8, depth), f32), ((2, planes, rows, 128), f32)],
        smem=range(1, 7),
        cost=1 << 20,
    )
    far = [None, None]
    e0 = [None, None]
    msg = [None, None]
    state = (e, h, p, j)
    keep = [state_shape] * 4
    e0_shape = ((2, 2) + ext, f32)
    side_edges = swap(edges, "gy", 0)
    size = 8 * rows + 16
    rec_shape = (rec.shape, f32)
    for which in ORDER:
        if which == ORDER[0]:
            ins = (cs, side_edges) + tables + state + (coef,)
            *state, coef, e0[which], out = call(
                lambda *refs, which=which: send_body(rows, which, True, 0, refs),
                ins,
                keep + [coef_shape, e0_shape, ((size + rows + EDGE, depth), f32)],
                {7 + i: i for i in range(5)},
                smem=range(2, 7),
            )
        else:
            *state, e0[which], out, rec = call(
                lambda *refs, which=which: send_body(rows, which, True, 0, refs),
                tuple(state) + (coef, rec),
                keep + [e0_shape, ((size + rows + EDGE, depth), f32), rec_shape],
                {0: 0, 1: 1, 2: 2, 3: 3, 5: 6},
            )
            out, msg[ORDER[0]] = lax.optimization_barrier((out, msg[ORDER[0]]))
        msg[which] = far[which] = swap(out, "gx", which)
    for step in range(0, STEPS, 2):
        final = step == STEPS - 2
        for which in ORDER:
            edge_shape = [] if final else [((tiles // 2, 8, depth), f32)]
            *state, rec = call(
                lambda *refs, which=which, step=step, final=final: finish_body(rows, which, step, final, refs),
                (cs, msg[which], e0[which], far[which], coef) + tuple(state) + (rec,),
                keep + [rec_shape] + edge_shape,
                {5 + i: i for i in range(5)},
            )
            if final:
                continue
            side_edges = swap(rec, "gy", 0)
            rec = state.pop()
            second = which == ORDER[1]
            *state, e0[which], out = call(
                lambda *refs, which=which, step=step: send_body(rows, which, False, step + 2, refs),
                (cs, side_edges) + tuple(state) + (coef,) + ((rec,) if second else ()),
                keep + [e0_shape, ((size, depth), f32)] + ([rec_shape] if second else []),
                {2: 0, 3: 1, 4: 2, 5: 3, **({7: 6} if second else {})},
            )
            if second:
                rec, out = out, e0[which]
                e0[which] = state.pop()
            msg[which] = swap(out, "gx", which)
            if second and step == STEPS - 4:
                *state, rec = call(
                    lambda *refs: inner_part(rows, STEPS - 2, refs[6:], refs[5]),
                    (*state, rec, coef),
                    keep + [rec_shape],
                    {i: i for i in range(5)},
                )
    e, h, p, j = state
    (harm,) = call(harmonics_body, (rec, waves), [((2, planes, HARM, 128), f32)])
    other = swap(harm, "gy", 0)
    fields = call(
        functools.partial(store_body, rows),
        (e, h, p, j),
        [(electric.shape, f32)] * 4,
        hbm_out=True,
        scratch=[pltpu.SemaphoreType.DMA((4,))],
        cost=1 << 22,
    )
    (panel,) = call(panel_body, (harm, other), [((2, STEPS, planes, HARM), f32)])
    return (*fields, jnp.transpose(panel, (0, 1, 3, 2)))


def solution(mesh):
    field = P("angle", None, "gx", "gy", None)
    in_specs = (field,) * 4 + (P("gx", "gy", None),) + (P(),) * 5 + (P("angle"),)
    out_specs = (field,) * 4 + (P("angle", None, None, "gx"),)
    return jax.shard_map(per_device, mesh=mesh, in_specs=in_specs, out_specs=out_specs, check_vma=False)
```
